512 devices in a mesh: blk: 16 (over y, x_lo), shard: 32 (over x_hi, z, core).
Axes of the slice: x: 4 (x_hi: 2, x_lo: 2; x = x_hi * 2 + x_lo), y: 8, z: 8, core: 2. Of those that a mesh axis runs over, the one named last changes fastest.
Arguments:
- queries: float32 [65536, 3584], P(('blk', 'shard')), may hold values from -0.25 to 0.25
- passages: float32 [4096, 3584], P(('blk', 'shard')), may hold values from -0.25 to 0.25
- positive: int32 [65536], P(('blk', 'shard')), may hold values from 0 to 127
- neg_owner: int32 [65536, 7], P(('blk', 'shard')), may hold values from 0 to 31, all different within a row; in each aligned block of 128 rows (0 to 127, 128 to 255, ...) at most 32 rows name the same one
- neg_row: int32 [65536, 7], P(('blk', 'shard')), may hold values from 0 to 7
Outputs:
- query_gradient: float32 [65536, 3584], P(('blk', 'shard'))
- passage_gradient: float32 [4096, 3584], P(('blk', 'shard'))
- losses: float32 [65536], P(('blk', 'shard'))
The draws below stay inside these ranges and needn't reach their ends.
Inputs may be any that keep to these rules, and one draw needn't show every extreme that they name: `neg_owner`: the 7 owners of one query are distinct; among the rows of one device no shard is named more than 32 times, and in some device's rows one shard is named exactly 32 times.
All inputs are finite; a program needn't handle non-finite values.
Results may differ from the reference program's by a relative error of at most 0.015.
Values may be sent and summed in bfloat16 or wider, within the bound.
A program may use at most 64 MiB of HBM per device.

```python
import math
import jax
import jax.numpy as jnp
import numpy as np
from jax import lax

EMBED_WIDTH = 3584
Q_DEV = 128
PASSAGES_LOCAL = 8
NEG = 7
CAP = 32
GROUP = 128
QUERY_TOTAL = 65536
PASSAGE_TOTAL = 4096
N_BLK = 16
N_SHARD = 32


def shared_parts(key):
    reach = jnp.sqrt(jnp.float32(0.225 / EMBED_WIDTH))
    topic = reach * jax.random.normal(jax.random.fold_in(key, 103), (N_BLK, EMBED_WIDTH), jnp.float32)
    spread = reach * jax.random.normal(jax.random.fold_in(key, 104), (N_BLK * N_SHARD, EMBED_WIDTH), jnp.float32)
    return (topic, spread)


def draw_passages(key, part):
    topic, spread = shared_parts(key)
    key = jax.random.fold_in(key, 1)
    device = jnp.arange(PASSAGE_TOTAL) // PASSAGES_LOCAL
    common = topic[device // N_SHARD] + spread[device]
    base = 0.04 * jax.random.normal(key, (PASSAGE_TOTAL, EMBED_WIDTH), jnp.float32)
    return jnp.clip(base + common, -0.24, 0.24)


def draw_queries(key, part):
    topic, spread = shared_parts(key)
    key = jax.random.fold_in(key, 2)
    rows = jnp.arange(QUERY_TOTAL)
    device = rows // Q_DEV
    common = topic[device // N_SHARD] - spread[device]
    base = 0.04 * jax.random.normal(key, (QUERY_TOTAL, EMBED_WIDTH), jnp.float32)
    return jnp.clip(base + common, -0.24, 0.24)


def touch_ends(drawn, rng, least, largest):
    longest = drawn.shape.index(max(drawn.shape))
    spots = []
    for shift in (0, 1):
        where = [jax.random.randint(jax.random.fold_in(rng, axis), (), 0, length) for axis, length in enumerate(drawn.shape)]
        where[longest] = (where[longest] + shift) % drawn.shape[longest]
        spots.append(tuple(where))
    return drawn.at[spots[0]].set(least).at[spots[1]].set(largest)


def shared_out(rng, own, number, rows, amount, top, limit, slope):
    sequence = jax.random.permutation(rng, amount)
    crowded, usual = shares(amount, rows * top, limit, slope, True), shares(amount, rows * top, limit, slope, False)
    places = jnp.arange(amount)

    def named(lengths, rotation):
        used = int((lengths > 0).sum())
        fixed = max(1, used // 4)
        passed = fixed + (places - fixed + rotation * (used - fixed)) % max(1, amount - fixed)
        return jnp.zeros((amount,), jnp.int32).at[sequence[jnp.where(places < fixed, places, passed)]].set(jnp.asarray(lengths, jnp.int32))

    lengths = jnp.where(number % 4 == 0, named(crowded, number // 4), named(usual, number - number // 4 - 1))
    mixed = jax.random.permutation(jax.random.fold_in(own, 3), amount)
    donor, taker = mixed[0:amount // 2 * 2:2], mixed[1:amount // 2 * 2:2]
    slack = jnp.minimum(lengths[donor] - 1, limit - lengths[taker]) // 2
    slack = jnp.where((donor == sequence[0]) | (taker == sequence[0]) | (lengths[taker] == 0), 0, jnp.maximum(slack, 0))
    passed = jax.random.randint(jax.random.fold_in(own, 4), (amount // 2,), 0, 1 << 20) % (slack + 1)
    lengths = lengths.at[donor].add(-passed).at[taker].add(passed)
    labels = jnp.searchsorted(jnp.cumsum(lengths), jnp.arange(rows * top), side="right").astype(jnp.int32)
    grid = labels.reshape(top, rows).T
    grid = grid[jax.random.permutation(jax.random.fold_in(own, 1), rows)]
    rotation = jax.random.randint(jax.random.fold_in(own, 2), (rows, 1), 0, top)
    return jnp.take_along_axis(grid, (jnp.arange(top)[None, :] + rotation) % top, axis=1)


def shares(number_of, total, most, skew, full):
    loads = [(1 << 20) // math.isqrt(standing ** skew) + 1 for standing in range(1, number_of + 1)]
    largest = most if full else min(most, max(-(-total // number_of), total * loads[0] // sum(loads)))
    least = 1 if total - largest >= number_of - 1 else 0
    counts, spare = [largest] + [least] * (number_of - 1), total - largest - least * (number_of - 1)
    while spare > 0:
        movable = [i for i in range(1, number_of) if counts[i] < largest] or [i for i in range(1, number_of) if counts[i] < most]
        pool, budget = sum([loads[i] for i in movable]), spare
        for i in movable:
            more = min(most - counts[i], max(1, budget * loads[i] // pool), spare)
            counts[i] = counts[i] + more
            spare = spare - more
    return np.array(counts)


def setup_inputs(seed: int = 0) -> dict:
    key_list = jax.random.split(jax.random.key(seed), 6)
    queries = draw_queries(jax.random.fold_in(key_list[5], 71), 0)
    passages = draw_passages(jax.random.fold_in(key_list[5], 71), 0)
    positive = touch_ends(jax.random.randint(key_list[2], (QUERY_TOTAL,), 0, GROUP), jax.random.fold_in(key_list[2], 1), 0, GROUP - 1).astype(jnp.int32)
    neg_owner_keys = jax.random.split(jax.random.fold_in(key_list[3], 1), QUERY_TOTAL // Q_DEV)
    neg_owner_turns = jax.random.permutation(jax.random.fold_in(key_list[3], 3), QUERY_TOTAL // Q_DEV)
    neg_owner = jax.vmap(lambda own, number: shared_out(jax.random.fold_in(key_list[3], 2), own, number, Q_DEV, N_SHARD, NEG, CAP, 1))(neg_owner_keys, neg_owner_turns).reshape((QUERY_TOTAL, NEG))
    neg_row = touch_ends(jax.random.randint(key_list[4], (QUERY_TOTAL, NEG), 0, PASSAGES_LOCAL), jax.random.fold_in(key_list[4], 1), 0, PASSAGES_LOCAL - 1).astype(jnp.int32)
    return dict(queries=queries, passages=passages, positive=positive, neg_owner=neg_owner, neg_row=neg_row)


SOFTMAX_TEMP = 0.05


def reference(queries, passages, positive, neg_owner, neg_row):
    query_block = queries.astype(jnp.bfloat16).reshape(N_BLK, N_SHARD, Q_DEV, EMBED_WIDTH)
    pb = passages.astype(jnp.bfloat16).reshape(N_BLK, N_SHARD, PASSAGES_LOCAL, EMBED_WIDTH)
    bank_index = (neg_owner * PASSAGES_LOCAL + neg_row).astype(jnp.int32).reshape(N_BLK, N_SHARD * Q_DEV, NEG)

    def group_scores(shard):
        query_matrix = lax.dynamic_index_in_dim(query_block, shard, 1, False).reshape(N_BLK * Q_DEV, EMBED_WIDTH)
        passage_matrix = lax.dynamic_index_in_dim(pb, shard, 1, False).reshape(GROUP, EMBED_WIDTH)
        return jnp.dot(query_matrix, passage_matrix.T, preferred_element_type=jnp.float32) / SOFTMAX_TEMP

    inbatch_scores = lax.map(group_scores, jnp.arange(N_SHARD))
    inbatch_scores = inbatch_scores.reshape(N_SHARD, N_BLK, Q_DEV, GROUP).transpose(1, 0, 2, 3)

    def hard_rows(block):
        bank = lax.dynamic_index_in_dim(pb, block, 0, False).reshape(N_SHARD * PASSAGES_LOCAL, EMBED_WIDTH)
        index = lax.dynamic_index_in_dim(bank_index, block, 0, False)
        return bank[index]

    def hard_scores(block):
        query_matrix = lax.dynamic_index_in_dim(query_block, block, 0, False).reshape(N_SHARD * Q_DEV, EMBED_WIDTH)
        emb = hard_rows(block)
        return jnp.einsum("kr,kfr->kf", query_matrix.astype(jnp.float32), emb.astype(jnp.float32),
                          precision=lax.Precision.HIGHEST) / SOFTMAX_TEMP

    hardneg_scores = lax.map(hard_scores, jnp.arange(N_BLK)).reshape(N_BLK, N_SHARD, Q_DEV, NEG)

    top = jnp.maximum(jnp.max(inbatch_scores, -1), jnp.max(hardneg_scores, -1))
    total = jnp.sum(jnp.exp(inbatch_scores - top[..., None]), -1) + jnp.sum(jnp.exp(hardneg_scores - top[..., None]), -1)
    lse = top + jnp.log(total)
    pos = positive.reshape(N_BLK, N_SHARD, Q_DEV)
    hit = jnp.arange(GROUP) == pos[..., None]
    chosen = jnp.sum(jnp.where(hit, inbatch_scores, jnp.float32(0.0)), -1)
    losses = (lse - chosen).reshape(QUERY_TOTAL)
    w_in = (jnp.exp(inbatch_scores - lse[..., None]) - hit.astype(jnp.float32)).astype(jnp.bfloat16)
    w_hn = jnp.exp(hardneg_scores - lse[..., None]).astype(jnp.bfloat16)

    def group_grads(shard):
        query_matrix = lax.dynamic_index_in_dim(query_block, shard, 1, False).reshape(N_BLK * Q_DEV, EMBED_WIDTH)
        passage_matrix = lax.dynamic_index_in_dim(pb, shard, 1, False).reshape(GROUP, EMBED_WIDTH)
        ws = lax.dynamic_index_in_dim(w_in, shard, 1, False).reshape(N_BLK * Q_DEV, GROUP)
        grad_q = jnp.dot(ws, passage_matrix, preferred_element_type=jnp.float32)
        grad_p = jnp.dot(ws.T, query_matrix, preferred_element_type=jnp.float32)
        return grad_q, grad_p

    query_grad_inbatch, passage_grad_inbatch = lax.map(group_grads, jnp.arange(N_SHARD))
    query_grad_inbatch = query_grad_inbatch.reshape(N_SHARD, N_BLK, Q_DEV, EMBED_WIDTH).transpose(1, 0, 2, 3)
    passage_grad_inbatch = passage_grad_inbatch.reshape(N_SHARD, N_BLK, PASSAGES_LOCAL, EMBED_WIDTH).transpose(1, 0, 2, 3)

    def hard_grads(block):
        query_matrix = lax.dynamic_index_in_dim(query_block, block, 0, False).reshape(N_SHARD * Q_DEV, EMBED_WIDTH)
        ws = lax.dynamic_index_in_dim(w_hn, block, 0, False).reshape(N_SHARD * Q_DEV, NEG)
        emb = hard_rows(block)
        grad_q = jnp.einsum("qj,qjd->qd", ws.astype(jnp.float32), emb.astype(jnp.float32),
                            precision=lax.Precision.HIGHEST)
        terms = ws.astype(jnp.float32)[:, :, None] * query_matrix.astype(jnp.float32)[:, None, :]
        source = (jnp.arange(N_SHARD * Q_DEV * NEG, dtype=jnp.int32) // (Q_DEV * NEG)).astype(jnp.int32)
        index = lax.dynamic_index_in_dim(bank_index, block, 0, False).reshape(-1) + source * (N_SHARD * PASSAGES_LOCAL)
        partial_sums = jax.ops.segment_sum(terms.reshape(-1, EMBED_WIDTH), index.astype(jnp.int32),
                                   num_segments=N_SHARD * N_SHARD * PASSAGES_LOCAL)
        part = (partial_sums / SOFTMAX_TEMP).astype(jnp.bfloat16).reshape(N_SHARD, N_SHARD * PASSAGES_LOCAL, EMBED_WIDTH)
        grad_p = jnp.sum(part.astype(jnp.float32), 0)
        return grad_q, grad_p

    query_grad_hardneg, passage_grad_hardneg = lax.map(hard_grads, jnp.arange(N_BLK))
    query_grad_hardneg = query_grad_hardneg.reshape(N_BLK, N_SHARD, Q_DEV, EMBED_WIDTH)
    passage_grad_hardneg = passage_grad_hardneg.reshape(N_BLK, N_SHARD, PASSAGES_LOCAL, EMBED_WIDTH)
    query_gradient = ((query_grad_inbatch + query_grad_hardneg) / SOFTMAX_TEMP).reshape(QUERY_TOTAL, EMBED_WIDTH)
    passage_gradient = (passage_grad_inbatch / SOFTMAX_TEMP + passage_grad_hardneg).reshape(PASSAGE_TOTAL, EMBED_WIDTH)
    return query_gradient, passage_gradient, losses
```

```python
import jax
import jax.numpy as jnp
from jax import lax
from jax.sharding import PartitionSpec as P

SOFTMAX_TEMP = 0.05


def body(queries, passages, positive, neg_owner, neg_row):
    nblk = lax.axis_size("blk")
    nshard = lax.axis_size("shard")
    qb = queries.astype(jnp.bfloat16)
    pb = passages.astype(jnp.bfloat16)
    rows_p, width = pb.shape
    group = nblk * rows_p
    bank_rows = nshard * rows_p
    bank = lax.all_gather(pb, "shard", axis=0, tiled=True)
    members = lax.all_gather(pb, "blk", axis=0, tiled=True)
    index = neg_owner * rows_p + neg_row
    columns = jnp.arange(bank_rows, dtype=jnp.int32)
    named = jnp.any(index[:, :, None] == columns[None, None, :], axis=1)
    hit = jnp.arange(group, dtype=jnp.int32)[None, :] == positive[:, None]
    s_hn = jnp.einsum("qd,pd->qp", qb, bank, preferred_element_type=jnp.float32) / SOFTMAX_TEMP
    s_in = jnp.einsum("qd,pd->qp", qb, members, preferred_element_type=jnp.float32) / SOFTMAX_TEMP
    s_hn = jnp.where(named, s_hn, -jnp.inf)
    top = jnp.maximum(jnp.max(s_in, -1), jnp.max(s_hn, -1))
    total = jnp.sum(jnp.exp(s_in - top[:, None]), -1) + jnp.sum(jnp.exp(s_hn - top[:, None]), -1)
    lse = top + jnp.log(total)
    losses = lse - jnp.sum(jnp.where(hit, s_in, jnp.float32(0.0)), -1)
    w_in = (jnp.exp(s_in - lse[:, None]) - hit.astype(jnp.float32)).astype(jnp.bfloat16)
    w_hn = jnp.exp(s_hn - lse[:, None]).astype(jnp.bfloat16)
    part = jnp.einsum("qc,qd->cd", w_hn, qb, preferred_element_type=jnp.float32) / SOFTMAX_TEMP
    term = jnp.einsum("qc,qd->cd", w_in, qb, preferred_element_type=jnp.float32) / SOFTMAX_TEMP
    hard_grad = lax.psum_scatter(part.astype(jnp.bfloat16), "shard", scatter_dimension=0, tiled=True)
    group_grad = lax.psum_scatter(term.astype(jnp.bfloat16), "blk", scatter_dimension=0, tiled=True)
    query_gradient = (
        jnp.einsum("qp,pd->qd", w_in, members, preferred_element_type=jnp.float32)
        + jnp.einsum("qp,pd->qd", w_hn, bank, preferred_element_type=jnp.float32)
    ) / SOFTMAX_TEMP
    passage_gradient = hard_grad.astype(jnp.float32) + group_grad.astype(jnp.float32)
    return (query_gradient, passage_gradient, losses)


def solution(mesh):
    rows = P(("blk", "shard"), None)
    flat = P(("blk", "shard"))
    return jax.shard_map(
        body,
        mesh=mesh,
        in_specs=(rows, rows, flat, rows, rows),
        out_specs=(rows, rows, flat),
        check_vma=False,
    )
```

```python
import functools

import jax
import jax.numpy as jnp
from jax import lax
from jax.experimental import pallas as pl
from jax.experimental.pallas import tpu as pltpu
from jax.sharding import PartitionSpec as P

SCALE = 20.0
NONE = -1e30
MESH = pl.DeviceIdType.MESH
F32, BF16, I32 = jnp.float32, jnp.bfloat16, jnp.int32


def stacked(wide):
    half = wide.shape[1] // 2
    return jnp.concatenate([wide[:, :half], wide[:, half:]], axis=0)


def gather_lists(n):
    half = n // 2
    plus = [list(range(n - 1, half - 1 + kind, -1)) for kind in (0, 1)]
    minus = [list(range(1, half + kind)) for kind in (0, 1)]
    return plus, minus


def scatter_lists(n):
    half = n // 2
    plus = [(half, 0)]
    for r in range(half - 1, 0, -1):
        plus += [(r, 1), (r, 0)]
    minus = []
    for r in range(half - 1, 0, -1):
        minus += [(r, 0), (r + 1, 1)]
    minus.append((1, 1))
    return plus, minus


def kernel(
    nblk, nshard,
    q_hbm, p_hbm, pos_ref, owner_ref, row_ref,
    qg_hbm, pg_ref, loss_ref,
    qf, pf, q2, hbuf, gbuf, bank, sh, sg, bias, codes, codes_in, lse_out, lse_in,
    part_h, part_g, hs, hr, gs, gr, xs, xr, qs, qr,
    local_sem, ag_s, ag_r, xa_s, xa_r, core_s, core_r, rs_s, rs_r, xb_s, xb_r,
):
    ny, nz = nblk // 2, nshard // 4
    b, s = lax.axis_index("blk"), lax.axis_index("shard")
    y, xl = lax.div(b, 2), lax.rem(b, 2)
    xh, z, c = lax.div(s, 2 * nz), lax.rem(lax.div(s, 2), nz), lax.rem(s, 2)

    def device(y_, xl_, xh_, z_, c_):
        return (y_ * 2 + xl_, xh_ * (2 * nz) + z_ * 2 + c_)

    next_z = device(y, xl, xh, lax.rem(z + 1, nz), c)
    prev_z = device(y, xl, xh, lax.rem(z + nz - 1, nz), c)
    next_y = device(lax.rem(y + 1, ny), xl, xh, z, c)
    prev_y = device(lax.rem(y + ny - 1, ny), xl, xh, z, c)
    other_xh = device(y, xl, 1 - xh, z, c)
    other_xl = device(y, 1 - xl, xh, z, c)
    other_core = device(y, xl, xh, z, 1 - c)
    rings = (
        (nz, (next_z, prev_z), hbuf, other_xh, hs, hr, part_h),
        (ny, (next_y, prev_y), gbuf, other_xl, gs, gr, part_g),
    )
    rows_q, width = qf.shape
    rows_h, rows_g = 16 * nz, 16 * ny
    wh = width // 2
    quarter = width // 4

    def send(src, dst, ssem, rsem, to):
        copy = pltpu.make_async_remote_copy(
            src_ref=src, dst_ref=dst, send_sem=ssem, recv_sem=rsem, device_id=to, device_id_type=MESH
        )
        copy.start()
        return copy

    sent = []
    p_copy = pltpu.make_async_copy(p_hbm, pf, local_sem.at[0])
    p_copy.start()
    q_copy = pltpu.make_async_copy(q_hbm, qf, local_sem.at[1])
    q_copy.start()
    barrier = pltpu.get_barrier_semaphore()
    for to in (next_z, prev_z, next_y, prev_y, other_xh, other_xl, other_core):
        pl.semaphore_signal(barrier, inc=1, device_id=to, device_id_type=MESH)
    p_copy.wait()
    mine = stacked(pf[...]).astype(BF16)
    hbuf[0, 0] = mine
    gbuf[0, 0] = mine
    pl.semaphore_wait(barrier, 7)

    arrive = [{}, {}]
    for i, (n, near, buf, cross, _, _, _) in enumerate(rings):
        arrive[i][(0, 1)] = send(buf.at[0, 0], buf.at[0, 1], xa_s.at[i], xa_r.at[i], cross)
    lists = [gather_lists(ring[0]) for ring in rings]

    def gather_send(i, d, kind, step):
        n, near, buf = rings[i][:3]
        slots = lists[i][d][kind]
        if step >= len(slots):
            return
        dst = slots[step]
        src = 0 if step == 0 else slots[step - 1]
        if (src, kind) != (0, 0) and (src, kind) not in done[i]:
            arrive[i][(src, kind)].wait_recv()
            done[i].add((src, kind))
        arrive[i][(dst, kind)] = send(
            buf.at[src, kind], buf.at[dst, kind], ag_s.at[i, dst, kind], ag_r.at[i, dst, kind], near[d]
        )

    done = [{(0, 0)}, {(0, 0)}]
    for i in (0, 1):
        for d in (0, 1):
            gather_send(i, d, 0, 0)

    q_copy.wait()
    q2[0:rows_q, :] = qf[...].astype(BF16)
    q_send = send(
        q2.at[pl.ds(0, rows_q)], q2.at[pl.ds(rows_q, rows_q)], core_s.at[0], core_r.at[0], other_core
    )
    for i in (0, 1):
        for d in (0, 1):
            gather_send(i, d, 1, 0)
    shift_z, shift_y = max(nz // 2 - 2, 0), max(ny // 2 - 2, 0)
    negs = owner_ref.shape[0]
    owner_t, row_t = owner_ref[...], row_ref[...]
    place = ((owner_t >> 1) - z + (nz + shift_z)) & (nz - 1)
    cross_bit = (owner_t >= 2 * nz).astype(I32) ^ xh
    column = place * 16 + cross_bit * 8 + row_t
    same_core = (owner_t & 1) == c
    codes[0, 0:negs, :] = jnp.where(same_core, column, -1)
    codes[1, 0:negs, :] = jnp.where(same_core, -1, column)
    codes[1, negs:8, :] = jnp.full((8 - negs, rows_q), -1, I32)
    code_send = send(codes.at[1], codes_in, core_s.at[1], core_r.at[1], other_core)
    sent += [q_send, code_send]
    row_ids = lax.broadcasted_iota(I32, (rows_h, rows_q), 0)

    def bias_of(code):
        named = row_ids == code[0:1, :]
        for k in range(1, negs):
            named = named | (row_ids == code[k : k + 1, :])
        return jnp.where(named, jnp.float32(0.0), jnp.float32(NONE))

    bias[:, 0:rows_q] = bias_of(codes[0, 0:negs, :])
    p = pos_ref[...]
    g_column = (((p >> 4) - y + (ny + shift_y)) & (ny - 1)) * 16 + (((p >> 3) & 1) ^ xl) * 8 + (p & 7)
    hit = lax.broadcasted_iota(I32, (rows_g, rows_q), 0) == g_column

    base = (0, rows_h)
    shifts = (shift_z, shift_y)

    def place_of(i, slot):
        return (slot + shifts[i]) % rings[i][0]

    def assemble(i, slot):
        buf = rings[i][2]
        for kind in (0, 1):
            if (slot, kind) not in done[i]:
                arrive[i][(slot, kind)].wait_recv()
                done[i].add((slot, kind))
        first, second = buf[slot, 0].astype(F32), buf[slot, 1].astype(F32)
        at = base[i] + 16 * place_of(i, slot)
        bank[at : at + 16, 0:wh] = jnp.concatenate([first[0:8], second[0:8]], axis=0).astype(BF16)
        bank[at : at + 16, wh:width] = jnp.concatenate([first[8:16], second[8:16]], axis=0).astype(BF16)

    def scores(i, start, stop):
        if stop <= start:
            return
        rows = bank[base[i] + 16 * start : base[i] + 16 * stop, :]
        queries = q2[...] if i == 0 else q2[0:rows_q, :]
        out = lax.dot_general(rows, queries, (((1,), (1,)), ((), ())), preferred_element_type=F32) * SCALE
        if i == 0:
            sh[16 * start : 16 * stop, :] = out
        else:
            sg[16 * start : 16 * stop, :] = out

    rounds = max(nz, ny) // 2
    for step in range(1, rounds):
        for kind in (0, 1):
            for i in (0, 1):
                for d in (0, 1):
                    gather_send(i, d, kind, step)
    early = [max(2 * (ring[0] // 2 - 2) + 1, 0) for ring in rings]
    for i in (0, 1):
        for at in range(early[i]):
            assemble(i, (at - shifts[i]) % rings[i][0])
    q_send.wait_recv()
    for i in (0, 1):
        scores(i, 0, early[i])
    code_send.wait_recv()
    bias[:, rows_q : 2 * rows_q] = bias_of(codes_in[...])
    for i in (0, 1):
        for at in range(early[i], rings[i][0]):
            assemble(i, (at - shifts[i]) % rings[i][0])
    for i in (0, 1):
        scores(i, early[i], rings[i][0])

    s_g = sg[...]
    s_h = sh[...] + bias[...]
    s_own, s_par = s_h[:, 0:rows_q], s_h[:, rows_q : 2 * rows_q]
    top_own = jnp.maximum(jnp.max(s_g, 0, keepdims=True), jnp.max(s_own, 0, keepdims=True))
    sum_own = jnp.sum(jnp.exp(s_g - top_own), 0, keepdims=True) + jnp.sum(
        jnp.exp(s_own - top_own), 0, keepdims=True
    )
    top_par = jnp.max(s_par, 0, keepdims=True)
    sum_par = jnp.sum(jnp.exp(s_par - top_par), 0, keepdims=True)
    lse_out[0:1, :] = top_own
    lse_out[1:2, :] = sum_own
    lse_out[2:3, :] = top_par
    lse_out[3:4, :] = sum_par
    lse_out[4:8, :] = jnp.zeros((4, rows_q), F32)
    lse_send = send(lse_out, lse_in, core_s.at[2], core_r.at[2], other_core)
    sent.append(lse_send)
    chosen = jnp.sum(jnp.where(hit, s_g, jnp.float32(0.0)), 0, keepdims=True)
    lse_send.wait_recv()

    def joined(top_a, sum_a, top_b, sum_b):
        top = jnp.maximum(top_a, top_b)
        return top + jnp.log(sum_a * jnp.exp(top_a - top) + sum_b * jnp.exp(top_b - top))

    lse = joined(top_own, sum_own, lse_in[2:3, :], lse_in[3:4, :])
    lse_par = joined(lse_in[0:1, :], lse_in[1:2, :], top_par, sum_par)
    loss_ref[...] = lse - chosen
    w_g = jnp.exp(s_g - lse) - hit.astype(F32)
    w_own = jnp.exp(s_own - lse)
    w_par = jnp.exp(s_par - lse_par)
    w_h = jnp.concatenate([w_own, w_par], axis=1).astype(BF16)
    w_gb = w_g.astype(BF16)

    out_lists = [scatter_lists(ring[0]) for ring in rings]
    coming = [{}, {}]

    def terms(h):
        cols = slice(h * wh, (h + 1) * wh)
        part_h[:, cols] = jnp.dot(w_h, q2[:, cols], preferred_element_type=F32) * SCALE
        part_g[:, cols] = jnp.dot(w_gb, q2[0:rows_q, cols], preferred_element_type=F32) * SCALE

    def own_term(i, slot, h):
        at = 16 * place_of(i, slot)
        return rings[i][6][at : at + 16, h * wh : (h + 1) * wh]

    def scatter_send(i, d, step):
        n, near, _, _, out, into, _ = rings[i]
        if step >= len(out_lists[i][d]):
            return
        r, h = out_lists[i][d][step]
        value = own_term(i, r if d == 0 else n - r, h)
        if (d, r, h) in coming[i]:
            coming[i][(d, r, h)].wait_recv()
            value = value + into[d, r, h].astype(F32)
        out[d, r, h] = value.astype(BF16)
        copy = send(
            out.at[d, r, h], into.at[d, r - 1, h], rs_s.at[i, d, r, h], rs_r.at[i, d, r - 1, h], near[d]
        )
        coming[i][(d, r - 1, h)] = copy
        sent.append(copy)

    def all_dirs(step):
        for i in (0, 1):
            for d in (0, 1):
                scatter_send(i, d, step)

    terms(0)
    if nz == 8 and ny == 8:
        all_dirs(0)
        terms(1)
    else:
        terms(1)
        all_dirs(0)
    all_dirs(1)
    w_par_q = jnp.transpose(w_par).astype(BF16)
    w_own_q = jnp.concatenate([jnp.transpose(w_own), jnp.transpose(w_g)], axis=1).astype(BF16)
    for h in (0, 1):
        cols = slice(h * wh, (h + 1) * wh)
        qs[:, cols] = (jnp.dot(w_par_q, bank[0:rows_h, cols], preferred_element_type=F32) * SCALE).astype(BF16)
    qg_send = send(qs, qr, core_s.at[3], core_r.at[3], other_core)
    sent.append(qg_send)
    all_dirs(2)
    for h in (0, 1):
        cols = slice(h * wh, (h + 1) * wh)
        qf[:, cols] = jnp.dot(w_own_q, bank[:, cols], preferred_element_type=F32) * SCALE
    all_dirs(3)
    qg_send.wait_recv()
    qf[...] = qf[...] + qr[...].astype(F32)
    qg_copy = pltpu.make_async_copy(qf, qg_hbm, local_sem.at[2])
    qg_copy.start()
    for step in range(4, max(len(l) for lists_ in out_lists for l in lists_)):
        all_dirs(step)

    crossing, totals = {}, {}
    for h in (0, 1):
        for i in (0, 1):
            total = own_term(i, 0, h)
            for d in (0, 1):
                if (d, 0, h) in coming[i]:
                    coming[i][(d, 0, h)].wait_recv()
                    total = total + rings[i][5][d, 0, h].astype(F32)
            xs[i, h] = stacked(total[8:16]).astype(BF16)
            crossing[i, h] = send(xs.at[i, h], xr.at[i, h], xb_s.at[i, h], xb_r.at[i, h], rings[i][3])
            sent.append(crossing[i, h])
            totals[i, h] = total[0:8]
    for h in (0, 1):
        total = totals[0, h] + totals[1, h]
        crossing[0, h].wait_recv()
        crossing[1, h].wait_recv()
        over = xr[0, h].astype(F32) + xr[1, h].astype(F32)
        pg_ref[:, h * wh : h * wh + quarter] = total[:, 0:quarter] + over[0:8]
        pg_ref[:, h * wh + quarter : (h + 1) * wh] = total[:, quarter:wh] + over[8:16]
    for i in (0, 1):
        for copy in arrive[i].values():
            copy.wait_send()
    for copy in sent:
        copy.wait_send()
    qg_copy.wait()


def body(queries, passages, positive, neg_owner, neg_row):
    nblk, nshard = lax.axis_size("blk"), lax.axis_size("shard")
    ny, nz = nblk // 2, nshard // 4
    rows_q, width = queries.shape
    rows_p = passages.shape[0]
    wh = width // 2
    vmem = pl.BlockSpec(memory_space=pltpu.VMEM)
    anywhere = pl.BlockSpec(memory_space=pl.ANY)
    dma = pltpu.SemaphoreType.DMA
    top = max(ny, nz)
    scratch = [
        pltpu.VMEM((rows_q, width), F32),
        pltpu.VMEM((rows_p, width), F32),
        pltpu.VMEM((2 * rows_q, width), BF16),
        pltpu.VMEM((nz, 2, 16, wh), BF16),
        pltpu.VMEM((ny, 2, 16, wh), BF16),
        pltpu.VMEM((16 * (nz + ny), width), BF16),
        pltpu.VMEM((16 * nz, 2 * rows_q), F32),
        pltpu.VMEM((16 * ny, rows_q), F32),
        pltpu.VMEM((16 * nz, 2 * rows_q), F32),
        pltpu.VMEM((2, 8, rows_q), I32),
        pltpu.VMEM((8, rows_q), I32),
        pltpu.VMEM((8, rows_q), F32),
        pltpu.VMEM((8, rows_q), F32),
        pltpu.VMEM((16 * nz, width), F32),
        pltpu.VMEM((16 * ny, width), F32),
        pltpu.VMEM((2, nz // 2 + 1, 2, 16, wh), BF16),
        pltpu.VMEM((2, nz // 2, 2, 16, wh), BF16),
        pltpu.VMEM((2, ny // 2 + 1, 2, 16, wh), BF16),
        pltpu.VMEM((2, ny // 2, 2, 16, wh), BF16),
        pltpu.VMEM((2, 2, 16, wh // 2), BF16),
        pltpu.VMEM((2, 2, 16, wh // 2), BF16),
        pltpu.VMEM((rows_q, width), BF16),
        pltpu.VMEM((rows_q, width), BF16),
        dma((3,)),
        dma((2, top, 2)), dma((2, top, 2)),
        dma((2,)), dma((2,)),
        dma((4,)), dma((4,)),
        dma((2, 2, top // 2 + 1, 2)), dma((2, 2, top // 2 + 1, 2)),
        dma((2, 2)), dma((2, 2)),
    ]
    qg, pg, loss = pl.pallas_call(
        functools.partial(kernel, nblk, nshard),
        out_shape=(
            jax.ShapeDtypeStruct((rows_q, width), F32),
            jax.ShapeDtypeStruct((rows_p, width), F32),
            jax.ShapeDtypeStruct((1, rows_q), F32),
        ),
        in_specs=[anywhere, anywhere, vmem, vmem, vmem],
        out_specs=(anywhere, vmem, vmem),
        scratch_shapes=scratch,
        compiler_params=pltpu.CompilerParams(
            collective_id=0, has_side_effects=True, vmem_limit_bytes=40 * 1024 * 1024
        ),
    )(queries, passages, positive.reshape(1, rows_q), neg_owner.T, neg_row.T)
    return (qg, pg, loss.reshape(rows_q))


def solution(mesh):
    rows = P(("blk", "shard"), None)
    flat = P(("blk", "shard"))
    return jax.shard_map(
        body,
        mesh=mesh,
        in_specs=(rows, rows, flat, rows, rows),
        out_specs=(rows, rows, flat),
        check_vma=False,
    )
```

```python
import functools

import jax
import jax.numpy as jnp
from jax import lax
from jax.experimental import pallas as pl
from jax.experimental.pallas import tpu as pltpu
from jax.sharding import PartitionSpec as P

SCALE = 20.0
NONE = -1e30
MESH = pl.DeviceIdType.MESH
F32, BF16, I32 = jnp.float32, jnp.bfloat16, jnp.int32


def stacked(wide):
    half = wide.shape[1] // 2
    return jnp.concatenate([wide[:, :half], wide[:, half:]], axis=0)


def tree(n, kind):
    half = n // 2
    direct = 2 if half > 2 else 1
    edges = []
    for d in range(direct, 0, -1):
        if d < half:
            edges += [(0, d), (0, -d)]
    for d in range(direct + 1, half):
        edges += [(1 - d, 1), (d - 1, -1)]
    edges.append((1 - half, 1) if kind == 0 else (half - 1, -1))
    return edges


def kernel(
    nblk, nshard,
    q_hbm, p_hbm, pos_hbm, owner_hbm, row_hbm,
    qg_ref, pg_ref, loss_ref,
    qf, pf, pos_ref, owner_ref, row_ref, q2, hbuf, gbuf, bank, sh, sg, bias, codes, codes_in, lse_out, lse_in,
    part_h, part_g, hs, hr, gs, gr, xs, xr, qs, qr,
    local_sem, ag_s, ag_r, xa_s, xa_r, core_s, core_r, rs_s, rs_r, xb_s, xb_r,
):
    ny, nz = nblk // 2, nshard // 4
    b, s = lax.axis_index("blk"), lax.axis_index("shard")
    y, xl = lax.div(b, 2), lax.rem(b, 2)
    xh, z, c = lax.div(s, 2 * nz), lax.rem(lax.div(s, 2), nz), lax.rem(s, 2)

    def device(y_, xl_, xh_, z_, c_):
        return (y_ * 2 + xl_, xh_ * (2 * nz) + z_ * 2 + c_)

    def along_z(jump):
        return device(y, xl, xh, lax.rem(z + (jump + nz), nz), c)

    def along_y(jump):
        return device(lax.rem(y + (jump + ny), ny), xl, xh, z, c)

    other_xh = device(y, xl, 1 - xh, z, c)
    other_xl = device(y, 1 - xl, xh, z, c)
    other_core = device(y, xl, xh, z, 1 - c)
    rings = (
        (nz, along_z, hbuf, other_xh, hs, hr, part_h),
        (ny, along_y, gbuf, other_xl, gs, gr, part_g),
    )
    trees = [[tree(ring[0], kind) for kind in (0, 1)] for ring in rings]
    partners = {}
    for i, (n, at, _, cross, _, _, _) in enumerate(rings):
        partners[i, 0] = cross
        for kind in (0, 1):
            for _, jump in trees[i][kind]:
                for way in (jump, -jump):
                    partners[i, 1 + way % n] = at(way)
    partners[2, 0] = other_core
    rows_q, width = qf.shape
    rows_h, rows_g = 16 * nz, 16 * ny
    wh = width // 2

    def send(src, dst, ssem, rsem, to):
        copy = pltpu.make_async_remote_copy(
            src_ref=src, dst_ref=dst, send_sem=ssem, recv_sem=rsem, device_id=to, device_id_type=MESH
        )
        copy.start()
        return copy

    sent = []
    p_copy = pltpu.make_async_copy(p_hbm, pf, local_sem.at[0])
    p_copy.start()
    q_copy = pltpu.make_async_copy(q_hbm, qf, local_sem.at[1])
    q_copy.start()
    index_copies = [
        pltpu.make_async_copy(src, dst, local_sem.at[3 + i])
        for i, (src, dst) in enumerate(((pos_hbm, pos_ref), (owner_hbm, owner_ref), (row_hbm, row_ref)))
    ]
    for copy in index_copies:
        copy.start()
    barrier = pltpu.get_barrier_semaphore()
    for to in partners.values():
        pl.semaphore_signal(barrier, inc=1, device_id=to, device_id_type=MESH)
    p_copy.wait()
    mine = stacked(pf[...]).astype(BF16)
    hbuf[0, 0] = mine
    gbuf[0, 0] = mine
    pl.semaphore_wait(barrier, len(partners))

    arrive = [{}, {}]
    done = [{(0, 0)}, {(0, 0)}]

    def arrived(i, slot, kind):
        if (slot, kind) not in done[i]:
            arrive[i][(slot, kind)].wait_recv()
            done[i].add((slot, kind))

    def gather_sends(i, kind, pick):
        n, at, buf = rings[i][:3]
        for slot, jump in trees[i][kind]:
            if not pick(slot):
                continue
            src, dst = slot % n, (slot - jump) % n
            arrived(i, src, kind)
            arrive[i][(dst, kind)] = send(
                buf.at[src, kind], buf.at[dst, kind], ag_s.at[i, dst, kind], ag_r.at[i, dst, kind], at(jump)
            )

    for i, (n, at, buf, cross, _, _, _) in enumerate(rings):
        arrive[i][(0, 1)] = send(buf.at[0, 0], buf.at[0, 1], xa_s.at[i], xa_r.at[i], cross)
    for i in (0, 1):
        gather_sends(i, 0, lambda slot: slot == 0)

    q_copy.wait()
    q2[0:rows_q, :] = qf[...].astype(BF16)
    q_send = send(
        q2.at[pl.ds(0, rows_q)], q2.at[pl.ds(rows_q, rows_q)], core_s.at[0], core_r.at[0], other_core
    )
    shift_z, shift_y = max(nz // 2 - 2, 0), max(ny // 2 - 2, 0)
    negs = owner_ref.shape[0]
    for copy in index_copies:
        copy.wait()
    owner_t, row_t = owner_ref[...], row_ref[...]
    place = ((owner_t >> 1) - z + (nz + shift_z)) & (nz - 1)
    cross_bit = (owner_t >= 2 * nz).astype(I32) ^ xh
    column = place * 16 + cross_bit * 8 + row_t
    same_core = (owner_t & 1) == c
    codes[0, 0:negs, :] = jnp.where(same_core, column, -1)
    codes[1, 0:negs, :] = jnp.where(same_core, -1, column)
    codes[1, negs:8, :] = jnp.full((8 - negs, rows_q), -1, I32)
    code_send = send(codes.at[1], codes_in, core_s.at[1], core_r.at[1], other_core)
    sent += [q_send, code_send]
    row_ids = lax.broadcasted_iota(I32, (rows_h, rows_q), 0)

    def bias_of(code):
        named = row_ids == code[0:1, :]
        for k in range(1, negs):
            named = named | (row_ids == code[k : k + 1, :])
        return jnp.where(named, jnp.float32(0.0), jnp.float32(NONE))

    bias[:, 0:rows_q] = bias_of(codes[0, 0:negs, :])
    p = pos_ref[...]
    g_column = (((p >> 4) - y + (ny + shift_y)) & (ny - 1)) * 16 + (((p >> 3) & 1) ^ xl) * 8 + (p & 7)
    hit = lax.broadcasted_iota(I32, (rows_g, rows_q), 0) == g_column

    base = (0, rows_h)
    shifts = (shift_z, shift_y)

    def place_of(i, slot):
        return (slot + shifts[i]) % rings[i][0]

    def assemble(i, slot):
        buf = rings[i][2]
        for kind in (0, 1):
            arrived(i, slot, kind)
        first, second = buf[slot, 0].astype(F32), buf[slot, 1].astype(F32)
        at = base[i] + 16 * place_of(i, slot)
        bank[at : at + 16, 0:wh] = jnp.concatenate([first[0:8], second[0:8]], axis=0).astype(BF16)
        bank[at : at + 16, wh:width] = jnp.concatenate([first[8:16], second[8:16]], axis=0).astype(BF16)

    def scores(i, start, stop):
        if stop <= start:
            return
        rows = bank[base[i] + 16 * start : base[i] + 16 * stop, :]
        queries = q2[...] if i == 0 else q2[0:rows_q, :]
        out = lax.dot_general(rows, queries, (((1,), (1,)), ((), ())), preferred_element_type=F32) * SCALE
        if i == 0:
            sh[16 * start : 16 * stop, :] = out
        else:
            sg[16 * start : 16 * stop, :] = out

    for kind, least, most in ((1, 0, 0), (0, 1, 2), (1, 1, 2), (0, 3, 9)):
        for i in (0, 1):
            gather_sends(i, kind, lambda slot: least <= abs(slot) <= most)
    early = [max(2 * (ring[0] // 2 - 2) + 1, 0) for ring in rings]
    for i in (0, 1):
        for at in range(early[i]):
            assemble(i, (at - shifts[i]) % rings[i][0])
    q_send.wait_recv()
    for i in (0, 1):
        scores(i, 0, early[i])
    for i in (0, 1):
        gather_sends(i, 1, lambda slot: abs(slot) >= 3)
    code_send.wait_recv()
    bias[:, rows_q : 2 * rows_q] = bias_of(codes_in[...])
    for i in (0, 1):
        for at in range(early[i], rings[i][0]):
            assemble(i, (at - shifts[i]) % rings[i][0])
    for i in (0, 1):
        scores(i, early[i], rings[i][0])

    s_g = sg[...]
    s_h = sh[...] + bias[...]
    s_own, s_par = s_h[:, 0:rows_q], s_h[:, rows_q : 2 * rows_q]
    top_own = jnp.maximum(jnp.max(s_g, 0, keepdims=True), jnp.max(s_own, 0, keepdims=True))
    sum_own = jnp.sum(jnp.exp(s_g - top_own), 0, keepdims=True) + jnp.sum(
        jnp.exp(s_own - top_own), 0, keepdims=True
    )
    top_par = jnp.max(s_par, 0, keepdims=True)
    sum_par = jnp.sum(jnp.exp(s_par - top_par), 0, keepdims=True)
    lse_out[0:1, :] = top_own
    lse_out[1:2, :] = sum_own
    lse_out[2:3, :] = top_par
    lse_out[3:4, :] = sum_par
    lse_out[4:8, :] = jnp.zeros((4, rows_q), F32)
    lse_send = send(lse_out, lse_in, core_s.at[2], core_r.at[2], other_core)
    sent.append(lse_send)
    chosen = jnp.sum(jnp.where(hit, s_g, jnp.float32(0.0)), 0, keepdims=True)
    lse_send.wait_recv()

    def joined(top_a, sum_a, top_b, sum_b):
        top = jnp.maximum(top_a, top_b)
        return top + jnp.log(sum_a * jnp.exp(top_a - top) + sum_b * jnp.exp(top_b - top))

    lse = joined(top_own, sum_own, lse_in[2:3, :], lse_in[3:4, :])
    lse_par = joined(lse_in[0:1, :], lse_in[1:2, :], top_par, sum_par)
    loss_ref[...] = lse - chosen
    w_g = jnp.exp(s_g - lse) - hit.astype(F32)
    w_own = jnp.exp(s_own - lse)
    w_par = jnp.exp(s_par - lse_par)
    w_h = jnp.concatenate([w_own, w_par], axis=1).astype(BF16)
    w_gb = w_g.astype(BF16)

    def terms(i):
        weights, queries = (w_h, q2[...]) if i == 0 else (w_gb, q2[0:rows_q, :])
        rings[i][6][...] = jnp.dot(weights, queries, preferred_element_type=F32) * SCALE

    coming = [{}, {}]

    def summed(i, kind, slot):
        n, _, _, _, _, into, own = rings[i]
        at = 16 * place_of(i, slot % n) + 8 * kind
        value = stacked(own[at : at + 8, :])
        for e, copy in coming[i].get((kind, slot % n), []):
            copy.wait_recv()
            value = value + into[kind, e].astype(F32)
        return value

    def scatter_sends(i, kind, pick):
        n, at, _, _, out, into, _ = rings[i]
        edges = trees[i][kind]
        for e in range(len(edges) - 1, -1, -1):
            slot, jump = edges[e]
            if not pick(slot, slot - jump):
                continue
            out[kind, e] = summed(i, kind, slot - jump).astype(BF16)
            copy = send(out.at[kind, e], into.at[kind, e], rs_s.at[i, kind, e], rs_r.at[i, kind, e], at(-jump))
            coming[i].setdefault((kind, slot % n), []).append((e, copy))
            sent.append(copy)

    for i in (0, 1):
        terms(i)
        for kind in (1, 0):
            scatter_sends(i, kind, lambda slot, dst: abs(dst) == rings[i][0] // 2)
        for kind in (1, 0):
            sign = -1 if kind == 1 else 1
            scatter_sends(i, kind, lambda slot, dst: dst == 3 * sign and rings[i][0] > 6)
    for i in (0, 1):
        for kind in (1, 0):
            scatter_sends(i, kind, lambda slot, dst: abs(dst) == 1 and rings[i][0] > 2)
    w_par_q = jnp.transpose(w_par).astype(BF16)
    w_own_q = jnp.concatenate([jnp.transpose(w_own), jnp.transpose(w_g)], axis=1).astype(BF16)
    for h in (0, 1):
        cols = slice(h * wh, (h + 1) * wh)
        qs[:, cols] = (jnp.dot(w_par_q, bank[0:rows_h, cols], preferred_element_type=F32) * SCALE).astype(BF16)
    qg_send = send(qs, qr, core_s.at[3], core_r.at[3], other_core)
    sent.append(qg_send)
    for kind in (1, 0):
        sign = 1 if kind == 1 else -1
        for i in (0, 1):
            scatter_sends(i, kind, lambda slot, dst: dst == 3 * sign and rings[i][0] > 6)
    for h in (0, 1):
        cols = slice(h * wh, (h + 1) * wh)
        qf[:, cols] = jnp.dot(w_own_q, bank[:, cols], preferred_element_type=F32) * SCALE
    for kind in (1, 0):
        sign = -1 if kind == 1 else 1
        for i in (0, 1):
            scatter_sends(i, kind, lambda slot, dst: dst == 2 * sign and rings[i][0] > 4)
    qg_send.wait_recv()
    qg_ref[...] = qf[...] + qr[...].astype(F32)
    for kind in (1, 0):
        sign = 1 if kind == 1 else -1
        for i in (0, 1):
            scatter_sends(i, kind, lambda slot, dst: dst == 2 * sign and rings[i][0] > 4)

    crossing = []
    for i in (0, 1):
        xs[i] = summed(i, 1, 0).astype(BF16)
        crossing.append(send(xs.at[i], xr.at[i], xb_s.at[i], xb_r.at[i], rings[i][3]))
    sent += crossing
    total = summed(0, 0, 0) + summed(1, 0, 0)
    for i in (0, 1):
        crossing[i].wait_recv()
        total = total + xr[i].astype(F32)
    pg_ref[:, 0:wh] = total[0:8]
    pg_ref[:, wh:width] = total[8:16]
    for i in (0, 1):
        for copy in arrive[i].values():
            copy.wait_send()
    for copy in sent:
        copy.wait_send()


def hand_over(*refs):
    count = len(refs) // 2
    sem = refs[-1]
    copies = [pltpu.make_async_copy(refs[i], refs[count + i], sem.at[i]) for i in range(count)]
    for copy in copies:
        copy.start()
    for copy in copies:
        copy.wait()


def body(queries, passages, positive, neg_owner, neg_row):
    nblk, nshard = lax.axis_size("blk"), lax.axis_size("shard")
    ny, nz = nblk // 2, nshard // 4
    rows_q, width = queries.shape
    rows_p = passages.shape[0]
    negs = neg_owner.shape[1]
    wh = width // 2
    vmem = pl.BlockSpec(memory_space=pltpu.VMEM)
    anywhere = pl.BlockSpec(memory_space=pl.ANY)
    hbm = pl.BlockSpec(memory_space=pltpu.HBM)
    dma = pltpu.SemaphoreType.DMA
    top = max(ny, nz)
    scratch = [
        pltpu.VMEM((rows_q, width), F32),
        pltpu.VMEM((rows_p, width), F32),
        pltpu.VMEM((1, rows_q), I32),
        pltpu.VMEM((negs, rows_q), I32),
        pltpu.VMEM((negs, rows_q), I32),
        pltpu.VMEM((2 * rows_q, width), BF16),
        pltpu.VMEM((nz, 2, 16, wh), BF16),
        pltpu.VMEM((ny, 2, 16, wh), BF16),
        pltpu.VMEM((16 * (nz + ny), width), BF16),
        pltpu.VMEM((16 * nz, 2 * rows_q), F32),
        pltpu.VMEM((16 * ny, rows_q), F32),
        pltpu.VMEM((16 * nz, 2 * rows_q), F32),
        pltpu.VMEM((2, 8, rows_q), I32),
        pltpu.VMEM((8, rows_q), I32),
        pltpu.VMEM((8, rows_q), F32),
        pltpu.VMEM((8, rows_q), F32),
        pltpu.VMEM((16 * nz, width), F32),
        pltpu.VMEM((16 * ny, width), F32),
        pltpu.VMEM((2, nz - 1, 16, wh), BF16),
        pltpu.VMEM((2, nz - 1, 16, wh), BF16),
        pltpu.VMEM((2, ny - 1, 16, wh), BF16),
        pltpu.VMEM((2, ny - 1, 16, wh), BF16),
        pltpu.VMEM((2, 16, wh), BF16),
        pltpu.VMEM((2, 16, wh), BF16),
        pltpu.VMEM((rows_q, width), BF16),
        pltpu.VMEM((rows_q, width), BF16),
        dma((6,)),
        dma((2, top, 2)), dma((2, top, 2)),
        dma((2,)), dma((2,)),
        dma((4,)), dma((4,)),
        dma((2, 2, top - 1)), dma((2, 2, top - 1)),
        dma((2,)), dma((2,)),
    ]
    inputs = (queries, passages, positive.reshape(1, rows_q), neg_owner.T, neg_row.T)
    qg, pg, loss = pl.pallas_call(
        functools.partial(kernel, nblk, nshard),
        out_shape=(
            pltpu.VMEM((rows_q, width), F32),
            pltpu.VMEM((rows_p, width), F32),
            pltpu.VMEM((1, rows_q), F32),
        ),
        in_specs=[hbm] * 5,
        out_specs=(vmem,) * 3,
        scratch_shapes=scratch,
        compiler_params=pltpu.CompilerParams(
            collective_id=0, has_side_effects=True, vmem_limit_bytes=40 * 1024 * 1024
        ),
    )(*[pltpu.with_memory_space_constraint(a, pltpu.HBM) for a in inputs])
    qg, pg, loss = pl.pallas_call(
        hand_over,
        out_shape=tuple(jax.ShapeDtypeStruct(a.shape, a.dtype) for a in (qg, pg, loss)),
        in_specs=[anywhere] * 3,
        out_specs=(hbm,) * 3,
        scratch_shapes=[dma((3,))],
    )(*[pltpu.with_memory_space_constraint(a, pltpu.VMEM) for a in (qg, pg, loss)])
    return (qg, pg, loss.reshape(rows_q))


def solution(mesh):
    rows = P(("blk", "shard"), None)
    flat = P(("blk", "shard"))
    return jax.shard_map(
        body,
        mesh=mesh,
        in_specs=(rows, rows, flat, rows, rows),
        out_specs=(rows, rows, flat),
        check_vma=False,
    )
```

```python
import functools

import jax
import jax.numpy as jnp
from jax import lax
from jax.experimental import pallas as pl
from jax.experimental.pallas import tpu as pltpu
from jax.sharding import PartitionSpec as P

SCALE = 20.0
NONE = -1e30
MESH = pl.DeviceIdType.MESH
F32, BF16, I32 = jnp.float32, jnp.bfloat16, jnp.int32


def stacked(wide):
    half = wide.shape[1] // 2
    return jnp.concatenate([wide[:, :half], wide[:, half:]], axis=0)


GATHER = (
    ((0, -2), (0, 0), 0, 2),
    ((0, 2), (0, 0), 0, -2),
    ((0, 1), (0, 0), 0, -1),
    ((1, 0), (0, 0), 1, 0),
    ((1, -1), (1, 0), 0, 1),
    ((1, 2), (1, 0), 0, -2),
    ((1, -2), (0, -2), 1, 0),
    ((0, -1), (0, -2), 0, -1),
    ((0, -3), (0, -2), 0, 1),
    ((0, 3), (0, 2), 0, -1),
    ((1, 1), (1, 0), 0, -1),
    ((0, 4), (0, -2), 0, 2),
    ((1, 4), (1, -2), 0, 2),
    ((1, -3), (0, -3), 1, 0),
    ((1, 3), (1, 2), 0, -1),
)
SCATTER = (
    ((1, 4), (0, 4), 1, 0),
    ((1, -3), (1, -2), 0, 1),
    ((1, 3), (1, 2), 0, -1),
    ((1, -1), (0, -1), 1, 0),
    ((0, 3), (0, 2), 0, -1),
    ((0, 1), (0, 2), 0, 1),
    ((1, 1), (1, 0), 0, -1),
    ((0, -3), (0, -2), 0, 1),
    ((0, 4), (0, -2), 0, 2),
    ((1, -2), (0, -2), 1, 0),
    ((1, 2), (1, 0), 0, -2),
    ((0, -1), (0, 0), 0, 1),
    ((0, 2), (0, 0), 0, -2),
    ((0, -2), (0, 0), 0, 2),
    ((1, 0), (0, 0), 1, 0),
)
PAIR = (((0, 1), (0, 0), 0, -1), ((1, 0), (0, 0), 1, 0), ((1, 1), (1, 0), 0, -1))


def table(n, scatter):
    rows = (SCATTER if scatter else GATHER) if n == 8 else (PAIR[::-1] if scatter else PAIR)
    return [((k, r % n), (pk, pr % n), cross, jump) for (k, r), (pk, pr), cross, jump in rows]


def kernel(
    nblk, nshard,
    q_hbm, p_hbm, pos_hbm, owner_hbm, row_hbm,
    qg_ref, pg_ref, loss_ref,
    qf, pf, pos_ref, owner_ref, row_ref, q2, hbuf, gbuf, bank, sh, sg, bias, codes, codes_in, lse_out, lse_in,
    part_h, part_g, hs, hr, gs, gr, qs, qr,
    local_sem, ag_s, ag_r, core_s, core_r, rs_s, rs_r,
):
    ny, nz = nblk // 2, nshard // 4
    b, s = lax.axis_index("blk"), lax.axis_index("shard")
    y, xl = lax.div(b, 2), lax.rem(b, 2)
    xh, z, c = lax.div(s, 2 * nz), lax.rem(lax.div(s, 2), nz), lax.rem(s, 2)

    def device(y_, xl_, xh_, z_, c_):
        return (y_ * 2 + xl_, xh_ * (2 * nz) + z_ * 2 + c_)

    def along_z(cross, jump):
        return device(y, xl, 1 - xh if cross else xh, lax.rem(z + (jump + nz), nz), c)

    def along_y(cross, jump):
        return device(lax.rem(y + (jump + ny), ny), 1 - xl if cross else xl, xh, z, c)

    other_core = device(y, xl, xh, z, 1 - c)
    rings = (
        (nz, along_z, hbuf, hs, hr, part_h, table(nz, False), table(nz, True)),
        (ny, along_y, gbuf, gs, gr, part_g, table(ny, False), table(ny, True)),
    )
    partners = {(2, 0, 0): other_core}
    for i, ring in enumerate(rings):
        for rows in ring[6:8]:
            for _, _, cross, jump in rows:
                for way in (jump, -jump):
                    partners[i, cross, way % ring[0]] = ring[1](cross, way)
    rows_q, width = qf.shape
    rows_h, rows_g = 16 * nz, 16 * ny
    wh = width // 2

    def send(src, dst, ssem, rsem, to):
        copy = pltpu.make_async_remote_copy(
            src_ref=src, dst_ref=dst, send_sem=ssem, recv_sem=rsem, device_id=to, device_id_type=MESH
        )
        copy.start()
        return copy

    sent = []
    p_copy = pltpu.make_async_copy(p_hbm, pf, local_sem.at[0])
    p_copy.start()
    q_copy = pltpu.make_async_copy(q_hbm, qf, local_sem.at[1])
    q_copy.start()
    index_copies = [
        pltpu.make_async_copy(src, dst, local_sem.at[3 + i])
        for i, (src, dst) in enumerate(((pos_hbm, pos_ref), (owner_hbm, owner_ref), (row_hbm, row_ref)))
    ]
    for copy in index_copies:
        copy.start()
    barrier = pltpu.get_barrier_semaphore()
    for to in partners.values():
        pl.semaphore_signal(barrier, inc=1, device_id=to, device_id_type=MESH)
    p_copy.wait()
    mine = stacked(pf[...]).astype(BF16)
    hbuf[0, 0] = mine
    gbuf[0, 0] = mine
    pl.semaphore_wait(barrier, len(partners))

    arrive = [{}, {}]
    done = [{(0, 0)}, {(0, 0)}]

    def arrived(i, node):
        if node not in done[i]:
            arrive[i][node].wait_recv()
            done[i].add(node)

    def gather_sends(start, stop):
        for e in range(start, stop):
            for i, ring in enumerate(rings):
                at, buf, rows = ring[1], ring[2], ring[6]
                if e >= len(rows):
                    continue
                (kind, slot), (from_kind, from_slot), cross, jump = rows[e]
                arrived(i, (from_kind, from_slot))
                arrive[i][kind, slot] = send(
                    buf.at[from_slot, from_kind],
                    buf.at[slot, kind],
                    ag_s.at[i, e],
                    ag_r.at[i, e],
                    at(cross, jump),
                )

    gather_sends(0, 4 if nz == 8 or ny == 8 else 2)

    q_copy.wait()
    q2[0:rows_q, :] = qf[...].astype(BF16)
    q_send = send(
        q2.at[pl.ds(0, rows_q)], q2.at[pl.ds(rows_q, rows_q)], core_s.at[0], core_r.at[0], other_core
    )
    shift_z, shift_y = max(nz // 2 - 2, 0), max(ny // 2 - 2, 0)
    negs = owner_ref.shape[0]
    for copy in index_copies:
        copy.wait()
    owner_t, row_t = owner_ref[...], row_ref[...]
    place = ((owner_t >> 1) - z + (nz + shift_z)) & (nz - 1)
    cross_bit = (owner_t >= 2 * nz).astype(I32) ^ xh
    column = place * 16 + cross_bit * 8 + row_t
    same_core = (owner_t & 1) == c
    codes[0, 0:negs, :] = jnp.where(same_core, column, -1)
    codes[1, 0:negs, :] = jnp.where(same_core, -1, column)
    codes[1, negs:8, :] = jnp.full((8 - negs, rows_q), -1, I32)
    code_send = send(codes.at[1], codes_in, core_s.at[1], core_r.at[1], other_core)
    sent += [q_send, code_send]
    row_ids = lax.broadcasted_iota(I32, (rows_h, rows_q), 0)

    def bias_of(code):
        named = row_ids == code[0:1, :]
        for k in range(1, negs):
            named = named | (row_ids == code[k : k + 1, :])
        return jnp.where(named, jnp.float32(0.0), jnp.float32(NONE))

    bias[:, 0:rows_q] = bias_of(codes[0, 0:negs, :])
    p = pos_ref[...]
    g_column = (((p >> 4) - y + (ny + shift_y)) & (ny - 1)) * 16 + (((p >> 3) & 1) ^ xl) * 8 + (p & 7)
    hit = lax.broadcasted_iota(I32, (rows_g, rows_q), 0) == g_column

    base = (0, rows_h)
    shifts = (shift_z, shift_y)

    def place_of(i, slot):
        return (slot + shifts[i]) % rings[i][0]

    def assemble(i, slot):
        buf = rings[i][2]
        for kind in (0, 1):
            arrived(i, (kind, slot))
        first, second = buf[slot, 0].astype(F32), buf[slot, 1].astype(F32)
        at = base[i] + 16 * place_of(i, slot)
        bank[at : at + 16, 0:wh] = jnp.concatenate([first[0:8], second[0:8]], axis=0).astype(BF16)
        bank[at : at + 16, wh:width] = jnp.concatenate([first[8:16], second[8:16]], axis=0).astype(BF16)

    def scores(i, start, stop):
        if stop <= start:
            return
        rows = bank[base[i] + 16 * start : base[i] + 16 * stop, :]
        queries = q2[...] if i == 0 else q2[0:rows_q, :]
        out = lax.dot_general(rows, queries, (((1,), (1,)), ((), ())), preferred_element_type=F32) * SCALE
        if i == 0:
            sh[16 * start : 16 * stop, :] = out
        else:
            sg[16 * start : 16 * stop, :] = out

    gather_sends(4 if nz == 8 or ny == 8 else 2, 15)
    early = [3 if ring[0] == 8 else 0 for ring in rings]
    for i in (0, 1):
        for at in range(early[i]):
            assemble(i, (at - shifts[i]) % rings[i][0])
    q_send.wait_recv()
    for i in (0, 1):
        scores(i, 0, early[i])
    code_send.wait_recv()
    bias[:, rows_q : 2 * rows_q] = bias_of(codes_in[...])
    for i in (0, 1):
        for at in range(early[i], rings[i][0]):
            assemble(i, (at - shifts[i]) % rings[i][0])
    for i in (0, 1):
        scores(i, early[i], rings[i][0])

    s_g = sg[...]
    s_h = sh[...] + bias[...]
    s_own, s_par = s_h[:, 0:rows_q], s_h[:, rows_q : 2 * rows_q]
    top_own = jnp.maximum(jnp.max(s_g, 0, keepdims=True), jnp.max(s_own, 0, keepdims=True))
    sum_own = jnp.sum(jnp.exp(s_g - top_own), 0, keepdims=True) + jnp.sum(
        jnp.exp(s_own - top_own), 0, keepdims=True
    )
    top_par = jnp.max(s_par, 0, keepdims=True)
    sum_par = jnp.sum(jnp.exp(s_par - top_par), 0, keepdims=True)
    lse_out[0:1, :] = top_own
    lse_out[1:2, :] = sum_own
    lse_out[2:3, :] = top_par
    lse_out[3:4, :] = sum_par
    lse_out[4:8, :] = jnp.zeros((4, rows_q), F32)
    lse_send = send(lse_out, lse_in, core_s.at[2], core_r.at[2], other_core)
    sent.append(lse_send)
    chosen = jnp.sum(jnp.where(hit, s_g, jnp.float32(0.0)), 0, keepdims=True)
    lse_send.wait_recv()

    def joined(top_a, sum_a, top_b, sum_b):
        top = jnp.maximum(top_a, top_b)
        return top + jnp.log(sum_a * jnp.exp(top_a - top) + sum_b * jnp.exp(top_b - top))

    lse = joined(top_own, sum_own, lse_in[2:3, :], lse_in[3:4, :])
    lse_par = joined(lse_in[0:1, :], lse_in[1:2, :], top_par, sum_par)
    loss_ref[...] = lse - chosen
    w_g = jnp.exp(s_g - lse) - hit.astype(F32)
    w_own = jnp.exp(s_own - lse)
    w_par = jnp.exp(s_par - lse_par)
    w_h = jnp.concatenate([w_own, w_par], axis=1).astype(BF16)
    w_gb = w_g.astype(BF16)

    def terms(i):
        weights, queries = (w_h, q2[...]) if i == 0 else (w_gb, q2[0:rows_q, :])
        rings[i][5][...] = jnp.dot(weights, queries, preferred_element_type=F32) * SCALE

    coming = [{}, {}]

    def summed(i, node):
        kind, slot = node
        into, own = rings[i][4:6]
        at = 16 * place_of(i, slot) + 8 * kind
        value = stacked(own[at : at + 8, :])
        for e, copy in coming[i].get(node, []):
            copy.wait_recv()
            value = value + into[e].astype(F32)
        return value

    def scatter_send(i, e):
        at, out, into, rows = rings[i][1], rings[i][3], rings[i][4], rings[i][7]
        if e >= len(rows):
            return
        node, parent, cross, jump = rows[e]
        out[e] = summed(i, node).astype(BF16)
        copy = send(out.at[e], into.at[e], rs_s.at[i, e], rs_r.at[i, e], at(cross, -jump))
        coming[i].setdefault(parent, []).append((e, copy))
        sent.append(copy)

    def scatter_sends(start, stop):
        for e in range(start, stop):
            for i in (0, 1):
                scatter_send(i, e)

    leaves = 8 if nz == 8 or ny == 8 else 1
    for i in (0, 1):
        terms(i)
        for e in range(leaves):
            scatter_send(i, e)
    w_par_q = jnp.transpose(w_par).astype(BF16)
    w_own_q = jnp.concatenate([jnp.transpose(w_own), jnp.transpose(w_g)], axis=1).astype(BF16)
    for h in (0, 1):
        cols = slice(h * wh, (h + 1) * wh)
        qs[:, cols] = (jnp.dot(w_par_q, bank[0:rows_h, cols], preferred_element_type=F32) * SCALE).astype(BF16)
    qg_send = send(qs, qr, core_s.at[3], core_r.at[3], other_core)
    sent.append(qg_send)
    scatter_sends(leaves, 10)
    for h in (0, 1):
        cols = slice(h * wh, (h + 1) * wh)
        qf[:, cols] = jnp.dot(w_own_q, bank[:, cols], preferred_element_type=F32) * SCALE
    scatter_sends(10, 13)
    qg_send.wait_recv()
    qg_ref[...] = qf[...] + qr[...].astype(F32)
    scatter_sends(13, 15)
    total = summed(0, (0, 0)) + summed(1, (0, 0))
    pg_ref[:, 0:wh] = total[0:8]
    pg_ref[:, wh:width] = total[8:16]
    for i in (0, 1):
        for copy in arrive[i].values():
            copy.wait_send()
    for copy in sent:
        copy.wait_send()


def hand_over(*refs):
    count = len(refs) // 2
    sem = refs[-1]
    copies = [pltpu.make_async_copy(refs[i], refs[count + i], sem.at[i]) for i in range(count)]
    for copy in copies:
        copy.start()
    for copy in copies:
        copy.wait()


def body(queries, passages, positive, neg_owner, neg_row):
    nblk, nshard = lax.axis_size("blk"), lax.axis_size("shard")
    ny, nz = nblk // 2, nshard // 4
    rows_q, width = queries.shape
    rows_p = passages.shape[0]
    negs = neg_owner.shape[1]
    wh = width // 2
    vmem = pl.BlockSpec(memory_space=pltpu.VMEM)
    anywhere = pl.BlockSpec(memory_space=pl.ANY)
    hbm = pl.BlockSpec(memory_space=pltpu.HBM)
    dma = pltpu.SemaphoreType.DMA
    top = max(ny, nz)
    scratch = [
        pltpu.VMEM((rows_q, width), F32),
        pltpu.VMEM((rows_p, width), F32),
        pltpu.VMEM((1, rows_q), I32),
        pltpu.VMEM((negs, rows_q), I32),
        pltpu.VMEM((negs, rows_q), I32),
        pltpu.VMEM((2 * rows_q, width), BF16),
        pltpu.VMEM((nz, 2, 16, wh), BF16),
        pltpu.VMEM((ny, 2, 16, wh), BF16),
        pltpu.VMEM((16 * (nz + ny), width), BF16),
        pltpu.VMEM((16 * nz, 2 * rows_q), F32),
        pltpu.VMEM((16 * ny, rows_q), F32),
        pltpu.VMEM((16 * nz, 2 * rows_q), F32),
        pltpu.VMEM((2, 8, rows_q), I32),
        pltpu.VMEM((8, rows_q), I32),
        pltpu.VMEM((8, rows_q), F32),
        pltpu.VMEM((8, rows_q), F32),
        pltpu.VMEM((16 * nz, width), F32),
        pltpu.VMEM((16 * ny, width), F32),
        pltpu.VMEM((2 * nz - 1, 16, wh), BF16),
        pltpu.VMEM((2 * nz - 1, 16, wh), BF16),
        pltpu.VMEM((2 * ny - 1, 16, wh), BF16),
        pltpu.VMEM((2 * ny - 1, 16, wh), BF16),
        pltpu.VMEM((rows_q, width), BF16),
        pltpu.VMEM((rows_q, width), BF16),
        dma((6,)),
        dma((2, 2 * top - 1)), dma((2, 2 * top - 1)),
        dma((4,)), dma((4,)),
        dma((2, 2 * top - 1)), dma((2, 2 * top - 1)),
    ]
    inputs = (queries, passages, positive.reshape(1, rows_q), neg_owner.T, neg_row.T)
    qg, pg, loss = pl.pallas_call(
        functools.partial(kernel, nblk, nshard),
        out_shape=(
            pltpu.VMEM((rows_q, width), F32),
            pltpu.VMEM((rows_p, width), F32),
            pltpu.VMEM((1, rows_q), F32),
        ),
        in_specs=[hbm] * 5,
        out_specs=(vmem,) * 3,
        scratch_shapes=scratch,
        compiler_params=pltpu.CompilerParams(
            collective_id=0, has_side_effects=True, vmem_limit_bytes=40 * 1024 * 1024
        ),
    )(*[pltpu.with_memory_space_constraint(a, pltpu.HBM) for a in inputs])
    qg, pg, loss = pl.pallas_call(
        hand_over,
        out_shape=tuple(jax.ShapeDtypeStruct(a.shape, a.dtype) for a in (qg, pg, loss)),
        in_specs=[anywhere] * 3,
        out_specs=(hbm,) * 3,
        scratch_shapes=[dma((3,))],
    )(*[pltpu.with_memory_space_constraint(a, pltpu.VMEM) for a in (qg, pg, loss)])
    return (qg, pg, loss.reshape(rows_q))


def solution(mesh):
    rows = P(("blk", "shard"), None)
    flat = P(("blk", "shard"))
    return jax.shard_map(
        body,
        mesh=mesh,
        in_specs=(rows, rows, flat, rows, rows),
        out_specs=(rows, rows, flat),
        check_vma=False,
    )
```

```python
import functools

import jax
import jax.numpy as jnp
from jax import lax
from jax.experimental import pallas as pl
from jax.experimental.pallas import tpu as pltpu
from jax.sharding import PartitionSpec as P

SCALE = 20.0
NONE = -1e30
MESH = pl.DeviceIdType.MESH
F32, BF16, I32 = jnp.float32, jnp.bfloat16, jnp.int32


def stacked(wide):
    half = wide.shape[1] // 2
    return jnp.concatenate([wide[:, :half], wide[:, half:]], axis=0)


GATHER = (
    ((0, 2), (0, 0), 0, -2),
    ((0, -2), (0, 0), 0, 2),
    ((1, 0), (0, 0), 1, 0),
    ((1, 2), (0, 2), 1, 0),
    ((0, 4), (0, 2), 0, -2),
    ((0, -3), (0, -2), 0, 1),
    ((1, -1), (1, 0), 0, 1),
    ((0, 1), (0, 2), 0, 1),
    ((1, 1), (1, 0), 0, -1),
    ((1, -2), (0, -2), 1, 0),
    ((0, -1), (0, 0), 0, 1),
    ((1, 3), (1, 2), 0, -1),
    ((1, 4), (1, 2), 0, -2),
    ((1, -3), (0, -3), 1, 0),
    ((0, 3), (0, 4), 0, 1),
)
SCATTER = (
    ((1, 3), (1, 2), 0, -1),
    ((1, 4), (0, 4), 1, 0),
    ((1, -3), (1, -2), 0, 1),
    ((1, 1), (0, 1), 1, 0),
    ((0, 3), (0, 1), 0, -2),
    ((0, -3), (0, -2), 0, 1),
    ((1, -1), (1, 0), 0, 1),
    ((0, 4), (0, 2), 0, -2),
    ((1, -2), (1, 0), 0, 2),
    ((1, 2), (0, 2), 1, 0),
    ((0, 1), (0, 0), 0, -1),
    ((0, -2), (0, 0), 0, 2),
    ((0, -1), (0, 0), 0, 1),
    ((0, 2), (0, 0), 0, -2),
    ((1, 0), (0, 0), 1, 0),
)
FIRST, LEAVES = 3, 7
PAIR = (((0, 1), (0, 0), 0, -1), ((1, 0), (0, 0), 1, 0), ((1, 1), (1, 0), 0, -1))


def table(n, scatter):
    rows = (SCATTER if scatter else GATHER) if n == 8 else (PAIR[::-1] if scatter else PAIR)
    return [((k, r % n), (pk, pr % n), cross, jump) for (k, r), (pk, pr), cross, jump in rows]


def kernel(
    nblk, nshard,
    q_hbm, p_hbm, pos_hbm, owner_hbm, row_hbm,
    qg_ref, pg_ref, loss_ref,
    qf, pf, pos_ref, owner_ref, row_ref, q2, hbuf, gbuf, bank, q2t, sc, bias, codes, codes_in, lse_out, lse_in,
    part, hs, hr, gs, gr, qs, qr,
    local_sem, ag_s, ag_r, core_s, core_r, rs_s, rs_r,
):
    ny, nz = nblk // 2, nshard // 4
    b, s = lax.axis_index("blk"), lax.axis_index("shard")
    y, xl = lax.div(b, 2), lax.rem(b, 2)
    xh, z, c = lax.div(s, 2 * nz), lax.rem(lax.div(s, 2), nz), lax.rem(s, 2)

    def device(y_, xl_, xh_, z_, c_):
        return (y_ * 2 + xl_, xh_ * (2 * nz) + z_ * 2 + c_)

    def along_z(cross, jump):
        return device(y, xl, 1 - xh if cross else xh, lax.rem(z + (jump + nz), nz), c)

    def along_y(cross, jump):
        return device(lax.rem(y + (jump + ny), ny), 1 - xl if cross else xl, xh, z, c)

    other_core = device(y, xl, xh, z, 1 - c)
    rings = (
        (nz, along_z, hbuf, hs, hr, table(nz, False), table(nz, True)),
        (ny, along_y, gbuf, gs, gr, table(ny, False), table(ny, True)),
    )
    partners = {(2, 0, 0): other_core}
    for i, ring in enumerate(rings):
        for rows in ring[5:7]:
            for _, _, cross, jump in rows:
                for way in (jump, -jump):
                    partners[i, cross, way % ring[0]] = ring[1](cross, way)
    rows_q, width = qf.shape
    rows_h, rows_g = 16 * nz, 16 * ny
    wh = width // 2

    def send(src, dst, ssem, rsem, to):
        copy = pltpu.make_async_remote_copy(
            src_ref=src, dst_ref=dst, send_sem=ssem, recv_sem=rsem, device_id=to, device_id_type=MESH
        )
        copy.start()
        return copy

    sent = []
    p_copy = pltpu.make_async_copy(p_hbm, pf, local_sem.at[0])
    p_copy.start()
    q_copy = pltpu.make_async_copy(q_hbm, qf, local_sem.at[1])
    q_copy.start()
    index_copies = [
        pltpu.make_async_copy(src, dst, local_sem.at[3 + i])
        for i, (src, dst) in enumerate(((pos_hbm, pos_ref), (owner_hbm, owner_ref), (row_hbm, row_ref)))
    ]
    for copy in index_copies:
        copy.start()
    barrier = pltpu.get_barrier_semaphore()
    for to in partners.values():
        pl.semaphore_signal(barrier, inc=1, device_id=to, device_id_type=MESH)
    p_copy.wait()
    mine = stacked(pf[...]).astype(BF16)
    hbuf[0, 0] = mine
    gbuf[0, 0] = mine
    pl.semaphore_wait(barrier, len(partners))

    arrive = [{}, {}]
    done = [{(0, 0)}, {(0, 0)}]

    def arrived(i, node):
        if node not in done[i]:
            arrive[i][node].wait_recv()
            done[i].add(node)

    def gather_sends(start, stop):
        for e in range(start, stop):
            for i, ring in enumerate(rings):
                at, buf, rows = ring[1], ring[2], ring[5]
                if e >= len(rows):
                    continue
                (kind, slot), (from_kind, from_slot), cross, jump = rows[e]
                arrived(i, (from_kind, from_slot))
                arrive[i][kind, slot] = send(
                    buf.at[from_slot, from_kind],
                    buf.at[slot, kind],
                    ag_s.at[i, e],
                    ag_r.at[i, e],
                    at(cross, jump),
                )

    first = FIRST if nz == 8 or ny == 8 else 2
    gather_sends(0, first)

    q_copy.wait()
    q2[0:rows_q, :] = qf[...].astype(BF16)
    q_send = send(
        q2.at[pl.ds(0, rows_q)], q2.at[pl.ds(rows_q, rows_q)], core_s.at[0], core_r.at[0], other_core
    )
    q2t[:, 0:rows_q] = jnp.transpose(q2[0:rows_q, :])
    shift_z, shift_y = max(nz // 2 - 2, 0), max(ny // 2 - 2, 0)
    negs = owner_ref.shape[0]
    for copy in index_copies:
        copy.wait()
    owner_t, row_t = owner_ref[...], row_ref[...]
    place = ((owner_t >> 1) - z + (nz + shift_z)) & (nz - 1)
    cross_bit = (owner_t >= 2 * nz).astype(I32) ^ xh
    column = place * 16 + cross_bit * 8 + row_t
    same_core = (owner_t & 1) == c
    codes[0, 0:negs, :] = jnp.where(same_core, column, -1)
    codes[1, 0:negs, :] = jnp.where(same_core, -1, column)
    codes[1, negs:8, :] = jnp.full((8 - negs, rows_q), -1, I32)
    code_send = send(codes.at[1], codes_in, core_s.at[1], core_r.at[1], other_core)
    sent += [q_send, code_send]
    row_ids = lax.broadcasted_iota(I32, (rows_h, rows_q), 0)

    def bias_of(code):
        named = row_ids == code[0:1, :]
        for k in range(1, negs):
            named = named | (row_ids == code[k : k + 1, :])
        return jnp.where(named, jnp.float32(0.0), jnp.float32(NONE))

    bias[:, 0:rows_q] = bias_of(codes[0, 0:negs, :])
    p = pos_ref[...]
    g_column = (((p >> 4) - y + (ny + shift_y)) & (ny - 1)) * 16 + (((p >> 3) & 1) ^ xl) * 8 + (p & 7)
    hit = lax.broadcasted_iota(I32, (rows_g, rows_q), 0) == g_column

    shifts = (shift_z, shift_y)
    early = [3 if ring[0] == 8 else 0 for ring in rings]
    first_late = 16 * (early[0] + early[1])
    starts = ((0, first_late), (16 * early[0], first_late + 16 * (nz - early[0])))

    def row_of(i, place):
        return starts[i][0] + 16 * place if place < early[i] else starts[i][1] + 16 * (place - early[i])

    def place_of(i, slot):
        return (slot + shifts[i]) % rings[i][0]

    def assemble(i, slot):
        buf = rings[i][2]
        for kind in (0, 1):
            arrived(i, (kind, slot))
        first, second = buf[slot, 0].astype(F32), buf[slot, 1].astype(F32)
        at = row_of(i, place_of(i, slot))
        bank[at : at + 16, 0:wh] = jnp.concatenate([first[0:8], second[0:8]], axis=0).astype(BF16)
        bank[at : at + 16, wh:width] = jnp.concatenate([first[8:16], second[8:16]], axis=0).astype(BF16)

    def scores(start, stop):
        if stop > start:
            sc[start:stop, :] = jnp.dot(bank[start:stop, :], q2t[...], preferred_element_type=F32) * SCALE

    gather_sends(first, 15)
    q_send.wait_recv()
    q2t[:, rows_q : 2 * rows_q] = jnp.transpose(q2[rows_q : 2 * rows_q, :])
    for i in (0, 1):
        for at in range(early[i]):
            assemble(i, (at - shifts[i]) % rings[i][0])
    scores(0, first_late)
    code_send.wait_recv()
    bias[:, rows_q : 2 * rows_q] = bias_of(codes_in[...])
    for i in (0, 1):
        for at in range(early[i], rings[i][0]):
            assemble(i, (at - shifts[i]) % rings[i][0])
    scores(first_late, rows_h + rows_g)

    def ring_rows(ref, i, cols):
        parts = [ref[starts[i][0] : starts[i][0] + 16 * early[i], cols]] if early[i] else []
        late = starts[i][1]
        return jnp.concatenate(parts + [ref[late : late + 16 * (rings[i][0] - early[i]), cols]], axis=0)

    s_g = ring_rows(sc, 1, slice(0, rows_q))
    s_h = ring_rows(sc, 0, slice(0, 2 * rows_q)) + bias[...]
    s_own, s_par = s_h[:, 0:rows_q], s_h[:, rows_q : 2 * rows_q]
    top_own = jnp.maximum(jnp.max(s_g, 0, keepdims=True), jnp.max(s_own, 0, keepdims=True))
    sum_own = jnp.sum(jnp.exp(s_g - top_own), 0, keepdims=True) + jnp.sum(
        jnp.exp(s_own - top_own), 0, keepdims=True
    )
    top_par = jnp.max(s_par, 0, keepdims=True)
    sum_par = jnp.sum(jnp.exp(s_par - top_par), 0, keepdims=True)
    lse_out[0:1, :] = top_own
    lse_out[1:2, :] = sum_own
    lse_out[2:3, :] = top_par
    lse_out[3:4, :] = sum_par
    lse_out[4:8, :] = jnp.zeros((4, rows_q), F32)
    lse_send = send(lse_out, lse_in, core_s.at[2], core_r.at[2], other_core)
    sent.append(lse_send)
    chosen = jnp.sum(jnp.where(hit, s_g, jnp.float32(0.0)), 0, keepdims=True)
    lse_send.wait_recv()

    def joined(top_a, sum_a, top_b, sum_b):
        top = jnp.maximum(top_a, top_b)
        return top + jnp.log(sum_a * jnp.exp(top_a - top) + sum_b * jnp.exp(top_b - top))

    lse = joined(top_own, sum_own, lse_in[2:3, :], lse_in[3:4, :])
    lse_par = joined(lse_in[0:1, :], lse_in[1:2, :], top_par, sum_par)
    loss_ref[...] = lse - chosen
    w_g = jnp.exp(s_g - lse) - hit.astype(F32)
    w_own = jnp.exp(s_own - lse)
    w_par = jnp.exp(s_par - lse_par)
    w_all = jnp.concatenate(
        [
            jnp.concatenate([w_own, w_par], axis=1),
            jnp.concatenate([w_g, jnp.zeros((rows_g, rows_q), F32)], axis=1),
        ],
        axis=0,
    ).astype(BF16)

    part[...] = jnp.dot(w_all, q2[...], preferred_element_type=F32) * SCALE

    coming = [{}, {}]

    def summed(i, node):
        kind, slot = node
        into = rings[i][4]
        at = i * rows_h + 16 * place_of(i, slot) + 8 * kind
        value = stacked(part[at : at + 8, :])
        for e, copy in coming[i].get(node, []):
            copy.wait_recv()
            value = value + into[e].astype(F32)
        return value

    def scatter_send(i, e):
        at, out, into, rows = rings[i][1], rings[i][3], rings[i][4], rings[i][6]
        if e >= len(rows):
            return
        node, parent, cross, jump = rows[e]
        out[e] = summed(i, node).astype(BF16)
        copy = send(out.at[e], into.at[e], rs_s.at[i, e], rs_r.at[i, e], at(cross, -jump))
        coming[i].setdefault(parent, []).append((e, copy))
        sent.append(copy)

    def scatter_sends(start, stop):
        for e in range(start, stop):
            for i in (0, 1):
                scatter_send(i, e)

    leaves = LEAVES if nz == 8 or ny == 8 else 1
    scatter_sends(0, leaves)
    settled = len(sent)
    def in_bank_order(of_h, of_g):
        cut_h, cut_g = 16 * early[0], 16 * early[1]
        parts = [of_h[0:cut_h]] * (cut_h > 0) + [of_g[0:cut_g]] * (cut_g > 0)
        return jnp.transpose(jnp.concatenate(parts + [of_h[cut_h:], of_g[cut_g:]], axis=0))

    w_q = jnp.concatenate(
        [in_bank_order(w_own, w_g), in_bank_order(w_par, jnp.zeros((rows_g, rows_q), F32))], axis=0
    ).astype(BF16)
    for h in (0, 1):
        cols = slice(h * wh, (h + 1) * wh)
        both = jnp.dot(w_q, bank[:, cols], preferred_element_type=F32) * SCALE
        qf[:, cols] = both[0:rows_q]
        qs[:, cols] = both[rows_q:].astype(BF16)
    qg_send = send(qs, qr, core_s.at[3], core_r.at[3], other_core)
    scatter_sends(leaves, max(leaves, 10))
    for i in (0, 1):
        for copy in arrive[i].values():
            copy.wait_send()
    for copy in sent[:settled]:
        copy.wait_send()
    scatter_sends(max(leaves, 10), 13)
    qg_send.wait_recv()
    qg_ref[...] = qf[...] + qr[...].astype(F32)
    scatter_sends(13, 15)
    total = summed(0, (0, 0)) + summed(1, (0, 0))
    pg_ref[:, 0:wh] = total[0:8]
    pg_ref[:, wh:width] = total[8:16]
    for copy in sent[settled:] + [qg_send]:
        copy.wait_send()


def hand_over(qg_in, pg_in, loss_in, qg, pg, loss, sem):
    pairs = ((qg_in, qg), (pg_in, pg), (loss_in, loss))
    copies = [pltpu.make_async_copy(src, dst, sem.at[i]) for i, (src, dst) in enumerate(pairs)]
    for copy in copies:
        copy.start()
    for copy in copies:
        copy.wait()


def body(queries, passages, positive, neg_owner, neg_row):
    nblk, nshard = lax.axis_size("blk"), lax.axis_size("shard")
    ny, nz = nblk // 2, nshard // 4
    rows_q, width = queries.shape
    rows_p = passages.shape[0]
    negs = neg_owner.shape[1]
    wh = width // 2
    vmem = pl.BlockSpec(memory_space=pltpu.VMEM)
    anywhere = pl.BlockSpec(memory_space=pl.ANY)
    hbm = pl.BlockSpec(memory_space=pltpu.HBM)
    dma = pltpu.SemaphoreType.DMA
    top = max(ny, nz)
    scratch = [
        pltpu.VMEM((rows_q, width), F32),
        pltpu.VMEM((rows_p, width), F32),
        pltpu.VMEM((1, rows_q), I32),
        pltpu.VMEM((negs, rows_q), I32),
        pltpu.VMEM((negs, rows_q), I32),
        pltpu.VMEM((2 * rows_q, width), BF16),
        pltpu.VMEM((nz, 2, 16, wh), BF16),
        pltpu.VMEM((ny, 2, 16, wh), BF16),
        pltpu.VMEM((16 * (nz + ny), width), BF16),
        pltpu.VMEM((width, 2 * rows_q), BF16),
        pltpu.VMEM((16 * (nz + ny), 2 * rows_q), F32),
        pltpu.VMEM((16 * nz, 2 * rows_q), F32),
        pltpu.VMEM((2, 8, rows_q), I32),
        pltpu.VMEM((8, rows_q), I32),
        pltpu.VMEM((8, rows_q), F32),
        pltpu.VMEM((8, rows_q), F32),
        pltpu.VMEM((16 * (nz + ny), width), F32),
        pltpu.VMEM((2 * nz - 1, 16, wh), BF16),
        pltpu.VMEM((2 * nz - 1, 16, wh), BF16),
        pltpu.VMEM((2 * ny - 1, 16, wh), BF16),
        pltpu.VMEM((2 * ny - 1, 16, wh), BF16),
        pltpu.VMEM((rows_q, width), BF16),
        pltpu.VMEM((rows_q, width), BF16),
        dma((6,)),
        dma((2, 2 * top - 1)), dma((2, 2 * top - 1)),
        dma((4,)), dma((4,)),
        dma((2, 2 * top - 1)), dma((2, 2 * top - 1)),
    ]
    inputs = (queries, passages, positive.reshape(1, rows_q), neg_owner.T, neg_row.T)
    qg, pg, loss = pl.pallas_call(
        functools.partial(kernel, nblk, nshard),
        out_shape=(
            pltpu.VMEM((rows_q, width), F32),
            pltpu.VMEM((rows_p, width), F32),
            pltpu.VMEM((1, rows_q), F32),
        ),
        in_specs=[hbm] * 5,
        out_specs=(vmem,) * 3,
        scratch_shapes=scratch,
        compiler_params=pltpu.CompilerParams(
            collective_id=0, has_side_effects=True, vmem_limit_bytes=40 * 1024 * 1024
        ),
    )(*[pltpu.with_memory_space_constraint(a, pltpu.HBM) for a in inputs])
    qg, pg, loss = pl.pallas_call(
        hand_over,
        out_shape=tuple(jax.ShapeDtypeStruct(a.shape, a.dtype) for a in (qg, pg, loss)),
        in_specs=[anywhere] * 3,
        out_specs=(hbm,) * 3,
        scratch_shapes=[dma((3,))],
    )(*[pltpu.with_memory_space_constraint(a, pltpu.VMEM) for a in (qg, pg, loss)])
    return (qg, pg, loss.reshape(rows_q))


def solution(mesh):
    rows = P(("blk", "shard"), None)
    flat = P(("blk", "shard"))
    return jax.shard_map(
        body,
        mesh=mesh,
        in_specs=(rows, rows, flat, rows, rows),
        out_specs=(rows, rows, flat),
        check_vma=False,
    )
```

```python
import functools

import jax
import jax.numpy as jnp
from jax import lax
from jax.experimental import pallas as pl
from jax.experimental.pallas import tpu as pltpu
from jax.sharding import PartitionSpec as P

SCALE = 20.0
NONE = -1e30
MESH = pl.DeviceIdType.MESH
F32, BF16, I32 = jnp.float32, jnp.bfloat16, jnp.int32


def stacked(wide):
    half = wide.shape[1] // 2
    return jnp.concatenate([wide[:, :half], wide[:, half:]], axis=0)


GATHER = (
    ((0, 2), (0, 0), 0, -2),
    ((0, -2), (0, 0), 0, 2),
    ((1, 0), (0, 0), 1, 0),
    ((1, 2), (0, 2), 1, 0),
    ((0, 4), (0, 2), 0, -2),
    ((0, -3), (0, -2), 0, 1),
    ((1, -1), (1, 0), 0, 1),
    ((0, 1), (0, 2), 0, 1),
    ((1, 1), (1, 0), 0, -1),
    ((1, -2), (0, -2), 1, 0),
    ((0, -1), (0, 0), 0, 1),
    ((1, 3), (1, 2), 0, -1),
    ((1, 4), (1, 2), 0, -2),
    ((1, -3), (0, -3), 1, 0),
    ((0, 3), (0, 4), 0, 1),
)
SCATTER = (
    ((1, 3), (1, 2), 0, -1),
    ((1, 4), (0, 4), 1, 0),
    ((1, -3), (1, -2), 0, 1),
    ((1, 1), (0, 1), 1, 0),
    ((0, 3), (0, 1), 0, -2),
    ((0, -3), (0, -2), 0, 1),
    ((1, -1), (1, 0), 0, 1),
    ((0, 4), (0, 2), 0, -2),
    ((1, -2), (1, 0), 0, 2),
    ((1, 2), (0, 2), 1, 0),
    ((0, 1), (0, 0), 0, -1),
    ((0, -2), (0, 0), 0, 2),
    ((0, -1), (0, 0), 0, 1),
    ((0, 2), (0, 0), 0, -2),
    ((1, 0), (0, 0), 1, 0),
)
FIRST, LEAVES = 3, 7
PAIR = (((0, 1), (0, 0), 0, -1), ((1, 0), (0, 0), 1, 0), ((1, 1), (1, 0), 0, -1))


def table(n, scatter):
    rows = (SCATTER if scatter else GATHER) if n == 8 else (PAIR[::-1] if scatter else PAIR)
    return [((k, r % n), (pk, pr % n), cross, jump) for (k, r), (pk, pr), cross, jump in rows]


def kernel(
    nblk, nshard,
    q_hbm, p_hbm, pos_hbm, owner_hbm, row_hbm,
    qg_ref, pg_ref, loss_ref,
    qf, pf, pos_ref, owner_ref, row_ref, q2, hbuf, gbuf, bank, q2t, sc, bias, codes, codes_in, lse_out, lse_in,
    part, hs, hr, gs, gr, qs, qr,
    local_sem, ag_s, ag_r, core_s, core_r, rs_s, rs_r,
):
    ny, nz = nblk // 2, nshard // 4
    b, s = lax.axis_index("blk"), lax.axis_index("shard")
    y, xl = lax.div(b, 2), lax.rem(b, 2)
    xh, z, c = lax.div(s, 2 * nz), lax.rem(lax.div(s, 2), nz), lax.rem(s, 2)

    def device(y_, xl_, xh_, z_, c_):
        return (y_ * 2 + xl_, xh_ * (2 * nz) + z_ * 2 + c_)

    def along_z(cross, jump):
        return device(y, xl, 1 - xh if cross else xh, lax.rem(z + (jump + nz), nz), c)

    def along_y(cross, jump):
        return device(lax.rem(y + (jump + ny), ny), 1 - xl if cross else xl, xh, z, c)

    other_core = device(y, xl, xh, z, 1 - c)
    rings = (
        (nz, along_z, hbuf, hs, hr, table(nz, False), table(nz, True)),
        (ny, along_y, gbuf, gs, gr, table(ny, False), table(ny, True)),
    )
    partners = {(2, 0, 0): other_core}
    for i, ring in enumerate(rings):
        for rows in ring[5:7]:
            for _, _, cross, jump in rows:
                for way in (jump, -jump):
                    partners[i, cross, way % ring[0]] = ring[1](cross, way)
    rows_q, width = qf.shape
    rows_h, rows_g = 16 * nz, 16 * ny
    wh = width // 2

    def send(src, dst, ssem, rsem, to):
        copy = pltpu.make_async_remote_copy(
            src_ref=src, dst_ref=dst, send_sem=ssem, recv_sem=rsem, device_id=to, device_id_type=MESH
        )
        copy.start()
        return copy

    sent = []
    p_copy = pltpu.make_async_copy(p_hbm, pf, local_sem.at[0])
    p_copy.start()
    barrier = pltpu.get_barrier_semaphore()
    for to in partners.values():
        pl.semaphore_signal(barrier, inc=1, device_id=to, device_id_type=MESH)
    q_copy = pltpu.make_async_copy(q_hbm, qf, local_sem.at[1])
    q_copy.start()
    index_copies = [
        pltpu.make_async_copy(src, dst, local_sem.at[3 + i])
        for i, (src, dst) in enumerate(((pos_hbm, pos_ref), (owner_hbm, owner_ref), (row_hbm, row_ref)))
    ]
    for copy in index_copies:
        copy.start()
    p_copy.wait()
    mine = stacked(pf[...]).astype(BF16)
    hbuf[0, 0] = mine
    gbuf[0, 0] = mine
    pl.semaphore_wait(barrier, len(partners))

    arrive = [{}, {}]
    done = [{(0, 0)}, {(0, 0)}]

    def arrived(i, node):
        if node not in done[i]:
            arrive[i][node].wait_recv()
            done[i].add(node)

    def gather_sends(start, stop):
        for e in range(start, stop):
            for i, ring in enumerate(rings):
                at, buf, rows = ring[1], ring[2], ring[5]
                if e >= len(rows):
                    continue
                (kind, slot), (from_kind, from_slot), cross, jump = rows[e]
                arrived(i, (from_kind, from_slot))
                arrive[i][kind, slot] = send(
                    buf.at[from_slot, from_kind],
                    buf.at[slot, kind],
                    ag_s.at[i, e],
                    ag_r.at[i, e],
                    at(cross, jump),
                )

    first = FIRST if nz == 8 or ny == 8 else 2
    gather_sends(0, first)

    q_copy.wait()
    q2[0:rows_q, :] = qf[...].astype(BF16)
    q_send = send(
        q2.at[pl.ds(0, rows_q)], q2.at[pl.ds(rows_q, rows_q)], core_s.at[0], core_r.at[0], other_core
    )
    shift_z, shift_y = max(nz // 2 - 2, 0), max(ny // 2 - 2, 0)
    negs = owner_ref.shape[0]
    for copy in index_copies:
        copy.wait()
    owner_t, row_t = owner_ref[...], row_ref[...]
    place = ((owner_t >> 1) - z + (nz + shift_z)) & (nz - 1)
    cross_bit = (owner_t >= 2 * nz).astype(I32) ^ xh
    column = place * 16 + cross_bit * 8 + row_t
    same_core = (owner_t & 1) == c
    codes[0, 0:negs, :] = jnp.where(same_core, column, -1)
    codes[1, 0:negs, :] = jnp.where(same_core, -1, column)
    codes[1, negs:8, :] = jnp.full((8 - negs, rows_q), -1, I32)
    code_send = send(codes.at[1], codes_in, core_s.at[1], core_r.at[1], other_core)
    sent += [q_send, code_send]
    row_ids = lax.broadcasted_iota(I32, (rows_h, rows_q), 0)

    def bias_of(code):
        named = row_ids == code[0:1, :]
        for k in range(1, negs):
            named = named | (row_ids == code[k : k + 1, :])
        return jnp.where(named, jnp.float32(0.0), jnp.float32(NONE))

    p = pos_ref[...]
    g_column = (((p >> 4) - y + (ny + shift_y)) & (ny - 1)) * 16 + (((p >> 3) & 1) ^ xl) * 8 + (p & 7)
    hit = lax.broadcasted_iota(I32, (rows_g, rows_q), 0) == g_column

    shifts = (shift_z, shift_y)
    early = [3 if ring[0] == 8 else 0 for ring in rings]
    first_late = 16 * (early[0] + early[1])
    starts = ((0, first_late), (16 * early[0], first_late + 16 * (nz - early[0])))

    def row_of(i, place):
        return starts[i][0] + 16 * place if place < early[i] else starts[i][1] + 16 * (place - early[i])

    def place_of(i, slot):
        return (slot + shifts[i]) % rings[i][0]

    def assemble(i, slot):
        buf = rings[i][2]
        for kind in (0, 1):
            arrived(i, (kind, slot))
        first, second = buf[slot, 0].astype(F32), buf[slot, 1].astype(F32)
        at = row_of(i, place_of(i, slot))
        bank[at : at + 16, 0:wh] = jnp.concatenate([first[0:8], second[0:8]], axis=0).astype(BF16)
        bank[at : at + 16, wh:width] = jnp.concatenate([first[8:16], second[8:16]], axis=0).astype(BF16)

    def scores(start, stop):
        if stop > start:
            sc[start:stop, :] = jnp.dot(bank[start:stop, :], q2t[...], preferred_element_type=F32) * SCALE

    gather_sends(first, 15)
    q_send.wait_recv()
    q2t[:, 0:rows_q] = jnp.transpose(q2[0:rows_q, :])
    q2t[:, rows_q : 2 * rows_q] = jnp.transpose(q2[rows_q : 2 * rows_q, :])
    for i in (0, 1):
        for at in range(early[i]):
            assemble(i, (at - shifts[i]) % rings[i][0])
    scores(0, first_late)
    code_send.wait_recv()
    bias[:, 0:rows_q] = bias_of(codes[0, 0:negs, :])
    bias[:, rows_q : 2 * rows_q] = bias_of(codes_in[...])
    late = [(at - shifts[i]) % ring[0] for i, ring in enumerate(rings) for at in range(early[i], ring[0])]
    for slot in sorted(set(late), key=lambda slot: (1, 2, 5, 4, 3, 0, 6, 7).index(slot)):
        for i in (0, 1):
            if slot < rings[i][0] and (slot + shifts[i]) % rings[i][0] >= early[i]:
                assemble(i, slot)
    scores(first_late, rows_h + rows_g)

    def ring_rows(ref, i, cols):
        parts = [ref[starts[i][0] : starts[i][0] + 16 * early[i], cols]] if early[i] else []
        late = starts[i][1]
        return jnp.concatenate(parts + [ref[late : late + 16 * (rings[i][0] - early[i]), cols]], axis=0)

    s_g = ring_rows(sc, 1, slice(0, rows_q))
    s_h = ring_rows(sc, 0, slice(0, 2 * rows_q)) + bias[...]
    s_own, s_par = s_h[:, 0:rows_q], s_h[:, rows_q : 2 * rows_q]
    top_own = jnp.maximum(jnp.max(s_g, 0, keepdims=True), jnp.max(s_own, 0, keepdims=True))
    sum_own = jnp.sum(jnp.exp(s_g - top_own), 0, keepdims=True) + jnp.sum(
        jnp.exp(s_own - top_own), 0, keepdims=True
    )
    top_par = jnp.max(s_par, 0, keepdims=True)
    sum_par = jnp.sum(jnp.exp(s_par - top_par), 0, keepdims=True)
    lse_out[0:1, :] = top_own
    lse_out[1:2, :] = sum_own
    lse_out[2:3, :] = top_par
    lse_out[3:4, :] = sum_par
    lse_out[4:8, :] = jnp.zeros((4, rows_q), F32)
    lse_send = send(lse_out, lse_in, core_s.at[2], core_r.at[2], other_core)
    sent.append(lse_send)
    chosen = jnp.sum(jnp.where(hit, s_g, jnp.float32(0.0)), 0, keepdims=True)
    lse_send.wait_recv()

    def joined(top_a, sum_a, top_b, sum_b):
        top = jnp.maximum(top_a, top_b)
        return top + jnp.log(sum_a * jnp.exp(top_a - top) + sum_b * jnp.exp(top_b - top))

    lse = joined(top_own, sum_own, lse_in[2:3, :], lse_in[3:4, :])
    lse_par = joined(lse_in[0:1, :], lse_in[1:2, :], top_par, sum_par)
    loss_ref[...] = lse - chosen
    w_g = jnp.exp(s_g - lse) - hit.astype(F32)
    w_own = jnp.exp(s_own - lse)
    w_par = jnp.exp(s_par - lse_par)
    w_all = jnp.concatenate(
        [
            jnp.concatenate([w_own, w_par], axis=1),
            jnp.concatenate([w_g, jnp.zeros((rows_g, rows_q), F32)], axis=1),
        ],
        axis=0,
    ).astype(BF16)

    part[...] = jnp.dot(w_all, q2[...], preferred_element_type=F32) * SCALE

    coming = [{}, {}]

    def summed(i, node):
        kind, slot = node
        into = rings[i][4]
        at = i * rows_h + 16 * place_of(i, slot) + 8 * kind
        value = stacked(part[at : at + 8, :])
        for e, copy in coming[i].get(node, []):
            copy.wait_recv()
            value = value + into[e].astype(F32)
        return value

    def scatter_send(i, e):
        at, out, into, rows = rings[i][1], rings[i][3], rings[i][4], rings[i][6]
        if e >= len(rows):
            return
        node, parent, cross, jump = rows[e]
        out[e] = summed(i, node).astype(BF16)
        copy = send(out.at[e], into.at[e], rs_s.at[i, e], rs_r.at[i, e], at(cross, -jump))
        coming[i].setdefault(parent, []).append((e, copy))
        sent.append(copy)

    def scatter_sends(start, stop):
        for e in range(start, stop):
            for i in (0, 1):
                scatter_send(i, e)

    leaves = LEAVES if nz == 8 or ny == 8 else 1
    scatter_sends(0, leaves)
    settled = len(sent)
    def in_bank_order(of_h, of_g):
        cut_h, cut_g = 16 * early[0], 16 * early[1]
        parts = [of_h[0:cut_h]] * (cut_h > 0) + [of_g[0:cut_g]] * (cut_g > 0)
        return jnp.transpose(jnp.concatenate(parts + [of_h[cut_h:], of_g[cut_g:]], axis=0))

    w_q = jnp.concatenate(
        [in_bank_order(w_own, w_g), in_bank_order(w_par, jnp.zeros((rows_g, rows_q), F32))], axis=0
    ).astype(BF16)

    def query_terms(h):
        cols = slice(h * wh, (h + 1) * wh)
        both = jnp.dot(w_q, bank[:, cols], preferred_element_type=F32) * SCALE
        qf[:, cols] = both[0:rows_q]
        qs[:, cols] = both[rows_q:].astype(BF16)

    scatter_sends(leaves, 9)
    query_terms(0)
    scatter_sends(max(leaves, 9), 10)
    query_terms(1)
    qg_send = send(qs, qr, core_s.at[3], core_r.at[3], other_core)
    scatter_sends(max(leaves, 10), 12)
    for i in (0, 1):
        for copy in arrive[i].values():
            copy.wait_send()
    for copy in sent[:settled]:
        copy.wait_send()
    scatter_sends(max(leaves, 12), 14)
    qg_send.wait_recv()
    qg_ref[...] = qf[...] + qr[...].astype(F32)
    scatter_sends(14, 15)
    total = summed(0, (0, 0)) + summed(1, (0, 0))
    pg_ref[:, 0:wh] = total[0:8]
    pg_ref[:, wh:width] = total[8:16]
    for copy in sent[settled:] + [qg_send]:
        copy.wait_send()


def hand_over(qg_in, pg_in, loss_in, qg, pg, loss, sem):
    pairs = ((qg_in, qg), (pg_in, pg), (loss_in, loss))
    copies = [pltpu.make_async_copy(src, dst, sem.at[i]) for i, (src, dst) in enumerate(pairs)]
    for copy in copies:
        copy.start()
    for copy in copies:
        copy.wait()


def body(queries, passages, positive, neg_owner, neg_row):
    nblk, nshard = lax.axis_size("blk"), lax.axis_size("shard")
    ny, nz = nblk // 2, nshard // 4
    rows_q, width = queries.shape
    rows_p = passages.shape[0]
    negs = neg_owner.shape[1]
    wh = width // 2
    vmem = pl.BlockSpec(memory_space=pltpu.VMEM)
    anywhere = pl.BlockSpec(memory_space=pl.ANY)
    hbm = pl.BlockSpec(memory_space=pltpu.HBM)
    dma = pltpu.SemaphoreType.DMA
    top = max(ny, nz)
    scratch = [
        pltpu.VMEM((rows_q, width), F32),
        pltpu.VMEM((rows_p, width), F32),
        pltpu.VMEM((1, rows_q), I32),
        pltpu.VMEM((negs, rows_q), I32),
        pltpu.VMEM((negs, rows_q), I32),
        pltpu.VMEM((2 * rows_q, width), BF16),
        pltpu.VMEM((nz, 2, 16, wh), BF16),
        pltpu.VMEM((ny, 2, 16, wh), BF16),
        pltpu.VMEM((16 * (nz + ny), width), BF16),
        pltpu.VMEM((width, 2 * rows_q), BF16),
        pltpu.VMEM((16 * (nz + ny), 2 * rows_q), F32),
        pltpu.VMEM((16 * nz, 2 * rows_q), F32),
        pltpu.VMEM((2, 8, rows_q), I32),
        pltpu.VMEM((8, rows_q), I32),
        pltpu.VMEM((8, rows_q), F32),
        pltpu.VMEM((8, rows_q), F32),
        pltpu.VMEM((16 * (nz + ny), width), F32),
        pltpu.VMEM((2 * nz - 1, 16, wh), BF16),
        pltpu.VMEM((2 * nz - 1, 16, wh), BF16),
        pltpu.VMEM((2 * ny - 1, 16, wh), BF16),
        pltpu.VMEM((2 * ny - 1, 16, wh), BF16),
        pltpu.VMEM((rows_q, width), BF16),
        pltpu.VMEM((rows_q, width), BF16),
        dma((6,)),
        dma((2, 2 * top - 1)), dma((2, 2 * top - 1)),
        dma((4,)), dma((4,)),
        dma((2, 2 * top - 1)), dma((2, 2 * top - 1)),
    ]
    inputs = (queries, passages, positive.reshape(1, rows_q), neg_owner.T, neg_row.T)
    qg, pg, loss = pl.pallas_call(
        functools.partial(kernel, nblk, nshard),
        out_shape=(
            pltpu.VMEM((rows_q, width), F32),
            pltpu.VMEM((rows_p, width), F32),
            pltpu.VMEM((1, rows_q), F32),
        ),
        in_specs=[hbm] * 5,
        out_specs=(vmem,) * 3,
        scratch_shapes=scratch,
        compiler_params=pltpu.CompilerParams(
            collective_id=0, has_side_effects=True, vmem_limit_bytes=40 * 1024 * 1024
        ),
    )(*[pltpu.with_memory_space_constraint(a, pltpu.HBM) for a in inputs])
    qg, pg, loss = pl.pallas_call(
        hand_over,
        out_shape=tuple(jax.ShapeDtypeStruct(a.shape, a.dtype) for a in (qg, pg, loss)),
        in_specs=[anywhere] * 3,
        out_specs=(hbm,) * 3,
        scratch_shapes=[dma((3,))],
    )(*[pltpu.with_memory_space_constraint(a, pltpu.VMEM) for a in (qg, pg, loss)])
    return (qg, pg, loss.reshape(rows_q))


def solution(mesh):
    rows = P(("blk", "shard"), None)
    flat = P(("blk", "shard"))
    return jax.shard_map(
        body,
        mesh=mesh,
        in_specs=(rows, rows, flat, rows, rows),
        out_specs=(rows, rows, flat),
        check_vma=False,
    )
```

```python
import functools

import jax
import jax.numpy as jnp
from jax import lax
from jax.experimental import pallas as pl
from jax.experimental.pallas import tpu as pltpu
from jax.sharding import PartitionSpec as P

SCALE = 20.0
NONE = -1e30
MESH = pl.DeviceIdType.MESH
F32, BF16, I32 = jnp.float32, jnp.bfloat16, jnp.int32


def stacked(wide):
    half = wide.shape[1] // 2
    return jnp.concatenate([wide[:, :half], wide[:, half:]], axis=0)


GATHER = (
    ((0, 2), (0, 0), 0, -2),
    ((0, -2), (0, 0), 0, 2),
    ((1, 0), (0, 0), 1, 0),
    ((1, 2), (0, 2), 1, 0),
    ((0, 4), (0, 2), 0, -2),
    ((0, -3), (0, -2), 0, 1),
    ((1, -1), (1, 0), 0, 1),
    ((0, 1), (0, 2), 0, 1),
    ((1, 1), (1, 0), 0, -1),
    ((1, -2), (0, -2), 1, 0),
    ((0, -1), (0, 0), 0, 1),
    ((1, 3), (1, 2), 0, -1),
    ((1, 4), (1, 2), 0, -2),
    ((1, -3), (0, -3), 1, 0),
    ((0, 3), (0, 4), 0, 1),
)
SCATTER = (
    ((1, 3), (1, 2), 0, -1),
    ((1, 4), (0, 4), 1, 0),
    ((1, -3), (1, -2), 0, 1),
    ((1, 1), (0, 1), 1, 0),
    ((0, 3), (0, 1), 0, -2),
    ((0, -3), (0, -2), 0, 1),
    ((1, -1), (1, 0), 0, 1),
    ((0, 4), (0, 2), 0, -2),
    ((1, -2), (1, 0), 0, 2),
    ((1, 2), (0, 2), 1, 0),
    ((0, 1), (0, 0), 0, -1),
    ((0, -2), (0, 0), 0, 2),
    ((0, -1), (0, 0), 0, 1),
    ((0, 2), (0, 0), 0, -2),
    ((1, 0), (0, 0), 1, 0),
)
FIRST, LEAVES = 3, 7
PAIR = (((0, 1), (0, 0), 0, -1), ((1, 0), (0, 0), 1, 0), ((1, 1), (1, 0), 0, -1))


def table(n, scatter):
    rows = (SCATTER if scatter else GATHER) if n == 8 else (PAIR[::-1] if scatter else PAIR)
    return [((k, r % n), (pk, pr % n), cross, jump) for (k, r), (pk, pr), cross, jump in rows]


def kernel(
    nblk, nshard,
    q_hbm, p_hbm, pos_hbm, owner_hbm, row_hbm,
    qg_ref, pg_ref, loss_ref,
    qf, pf, pos_ref, owner_ref, row_ref, q2, hbuf, gbuf, bank, q2t, sc, bias, codes, codes_in, lse_out, lse_in,
    part, hs, hr, gs, gr, qs, qr,
    local_sem, ag_s, ag_r, core_s, core_r, rs_s, rs_r,
):
    ny, nz = nblk // 2, nshard // 4
    b, s = lax.axis_index("blk"), lax.axis_index("shard")
    y, xl = lax.div(b, 2), lax.rem(b, 2)
    xh, z, c = lax.div(s, 2 * nz), lax.rem(lax.div(s, 2), nz), lax.rem(s, 2)

    def device(y_, xl_, xh_, z_, c_):
        return (y_ * 2 + xl_, xh_ * (2 * nz) + z_ * 2 + c_)

    def along_z(cross, jump):
        return device(y, xl, 1 - xh if cross else xh, lax.rem(z + (jump + nz), nz), c)

    def along_y(cross, jump):
        return device(lax.rem(y + (jump + ny), ny), 1 - xl if cross else xl, xh, z, c)

    other_core = device(y, xl, xh, z, 1 - c)
    rings = (
        (nz, along_z, hbuf, hs, hr, table(nz, False), table(nz, True)),
        (ny, along_y, gbuf, gs, gr, table(ny, False), table(ny, True)),
    )
    partners = {(2, 0, 0): other_core}
    for i, ring in enumerate(rings):
        for rows in ring[5:7]:
            for _, _, cross, jump in rows:
                for way in (jump, -jump):
                    partners[i, cross, way % ring[0]] = ring[1](cross, way)
    rows_q, width = qf.shape
    rows_h, rows_g = 16 * nz, 16 * ny
    wh = width // 2

    def send(src, dst, ssem, rsem, to):
        copy = pltpu.make_async_remote_copy(
            src_ref=src, dst_ref=dst, send_sem=ssem, recv_sem=rsem, device_id=to, device_id_type=MESH
        )
        copy.start()
        return copy

    sent = []
    p_copy = pltpu.make_async_copy(p_hbm, pf, local_sem.at[0])
    p_copy.start()
    q_copy = pltpu.make_async_copy(q_hbm, qf, local_sem.at[1])
    q_copy.start()
    index_copies = [
        pltpu.make_async_copy(src, dst, local_sem.at[3 + i])
        for i, (src, dst) in enumerate(((pos_hbm, pos_ref), (owner_hbm, owner_ref), (row_hbm, row_ref)))
    ]
    for copy in index_copies:
        copy.start()
    barrier = pltpu.get_barrier_semaphore()
    for to in partners.values():
        pl.semaphore_signal(barrier, inc=1, device_id=to, device_id_type=MESH)
    p_copy.wait()
    mine = stacked(pf[...]).astype(BF16)
    hbuf[0, 0] = mine
    gbuf[0, 0] = mine
    pl.semaphore_wait(barrier, len(partners))

    arrive = [{}, {}]
    done = [{(0, 0)}, {(0, 0)}]

    def arrived(i, node):
        if node not in done[i]:
            arrive[i][node].wait_recv()
            done[i].add(node)

    def gather_sends(start, stop):
        for e in range(start, stop):
            for i, ring in enumerate(rings):
                at, buf, rows = ring[1], ring[2], ring[5]
                if e >= len(rows):
                    continue
                (kind, slot), (from_kind, from_slot), cross, jump = rows[e]
                arrived(i, (from_kind, from_slot))
                arrive[i][kind, slot] = send(
                    buf.at[from_slot, from_kind],
                    buf.at[slot, kind],
                    ag_s.at[i, e],
                    ag_r.at[i, e],
                    at(cross, jump),
                )

    first = FIRST if nz == 8 or ny == 8 else 2
    gather_sends(0, first)

    q_copy.wait()
    q2[0:rows_q, :] = qf[...].astype(BF16)
    q_send = send(
        q2.at[pl.ds(0, rows_q)], q2.at[pl.ds(rows_q, rows_q)], core_s.at[0], core_r.at[0], other_core
    )
    shift_z, shift_y = max(nz // 2 - 2, 0), max(ny // 2 - 2, 0)
    negs = owner_ref.shape[0]
    for copy in index_copies:
        copy.wait()
    owner_t, row_t = owner_ref[...], row_ref[...]
    place = ((owner_t >> 1) - z + (nz + shift_z)) & (nz - 1)
    cross_bit = (owner_t >= 2 * nz).astype(I32) ^ xh
    column = place * 16 + cross_bit * 8 + row_t
    same_core = (owner_t & 1) == c
    codes[0, 0:negs, :] = jnp.where(same_core, column, -1)
    codes[1, 0:negs, :] = jnp.where(same_core, -1, column)
    codes[1, negs:8, :] = jnp.full((8 - negs, rows_q), -1, I32)
    code_send = send(codes.at[1], codes_in, core_s.at[1], core_r.at[1], other_core)
    sent += [q_send, code_send]
    row_ids = lax.broadcasted_iota(I32, (rows_h, rows_q), 0)

    def bias_of(code):
        named = row_ids == code[0:1, :]
        for k in range(1, negs):
            named = named | (row_ids == code[k : k + 1, :])
        return jnp.where(named, jnp.float32(0.0), jnp.float32(NONE))

    p = pos_ref[...]
    g_column = (((p >> 4) - y + (ny + shift_y)) & (ny - 1)) * 16 + (((p >> 3) & 1) ^ xl) * 8 + (p & 7)
    hit = lax.broadcasted_iota(I32, (rows_g, rows_q), 0) == g_column

    shifts = (shift_z, shift_y)
    early = [3 if ring[0] == 8 else 0 for ring in rings]
    first_late = 16 * (early[0] + early[1])
    starts = ((0, first_late), (16 * early[0], first_late + 16 * (nz - early[0])))

    def row_of(i, place):
        return starts[i][0] + 16 * place if place < early[i] else starts[i][1] + 16 * (place - early[i])

    def place_of(i, slot):
        return (slot + shifts[i]) % rings[i][0]

    def assemble(i, slot):
        buf = rings[i][2]
        for kind in (0, 1):
            arrived(i, (kind, slot))
        first, second = buf[slot, 0].astype(F32), buf[slot, 1].astype(F32)
        at = row_of(i, place_of(i, slot))
        bank[at : at + 16, 0:wh] = jnp.concatenate([first[0:8], second[0:8]], axis=0).astype(BF16)
        bank[at : at + 16, wh:width] = jnp.concatenate([first[8:16], second[8:16]], axis=0).astype(BF16)

    def scores(start, stop):
        if stop > start:
            sc[start:stop, :] = jnp.dot(bank[start:stop, :], q2t[...], preferred_element_type=F32) * SCALE

    gather_sends(first, 15)
    q_send.wait_recv()
    q2t[:, 0:rows_q] = jnp.transpose(q2[0:rows_q, :])
    q2t[:, rows_q : 2 * rows_q] = jnp.transpose(q2[rows_q : 2 * rows_q, :])
    for i in (0, 1):
        for at in range(early[i]):
            assemble(i, (at - shifts[i]) % rings[i][0])
    scores(0, first_late)
    code_send.wait_recv()
    bias[:, 0:rows_q] = bias_of(codes[0, 0:negs, :])
    bias[:, rows_q : 2 * rows_q] = bias_of(codes_in[...])
    for i in (0, 1):
        for at in range(early[i], rings[i][0]):
            assemble(i, (at - shifts[i]) % rings[i][0])
    scores(first_late, rows_h + rows_g)

    def ring_rows(ref, i, cols):
        parts = [ref[starts[i][0] : starts[i][0] + 16 * early[i], cols]] if early[i] else []
        late = starts[i][1]
        return jnp.concatenate(parts + [ref[late : late + 16 * (rings[i][0] - early[i]), cols]], axis=0)

    s_g = ring_rows(sc, 1, slice(0, rows_q))
    s_h = ring_rows(sc, 0, slice(0, 2 * rows_q)) + bias[...]
    s_own, s_par = s_h[:, 0:rows_q], s_h[:, rows_q : 2 * rows_q]
    top_own = jnp.maximum(jnp.max(s_g, 0, keepdims=True), jnp.max(s_own, 0, keepdims=True))
    sum_own = jnp.sum(jnp.exp(s_g - top_own), 0, keepdims=True) + jnp.sum(
        jnp.exp(s_own - top_own), 0, keepdims=True
    )
    top_par = jnp.max(s_par, 0, keepdims=True)
    sum_par = jnp.sum(jnp.exp(s_par - top_par), 0, keepdims=True)
    lse_out[0:1, :] = top_own
    lse_out[1:2, :] = sum_own
    lse_out[2:3, :] = top_par
    lse_out[3:4, :] = sum_par
    lse_out[4:8, :] = jnp.zeros((4, rows_q), F32)
    lse_send = send(lse_out, lse_in, core_s.at[2], core_r.at[2], other_core)
    sent.append(lse_send)
    chosen = jnp.sum(jnp.where(hit, s_g, jnp.float32(0.0)), 0, keepdims=True)
    lse_send.wait_recv()

    def joined(top_a, sum_a, top_b, sum_b):
        top = jnp.maximum(top_a, top_b)
        return top + jnp.log(sum_a * jnp.exp(top_a - top) + sum_b * jnp.exp(top_b - top))

    lse = joined(top_own, sum_own, lse_in[2:3, :], lse_in[3:4, :])
    lse_par = joined(lse_in[0:1, :], lse_in[1:2, :], top_par, sum_par)
    loss_ref[...] = lse - chosen
    w_g = jnp.exp(s_g - lse) - hit.astype(F32)
    w_own = jnp.exp(s_own - lse)
    w_par = jnp.exp(s_par - lse_par)
    w_all = jnp.concatenate(
        [
            jnp.concatenate([w_own, w_par], axis=1),
            jnp.concatenate([w_g, jnp.zeros((rows_g, rows_q), F32)], axis=1),
        ],
        axis=0,
    ).astype(BF16)

    part[...] = jnp.dot(w_all, q2[...], preferred_element_type=F32) * SCALE

    coming = [{}, {}]

    def summed(i, node):
        kind, slot = node
        into = rings[i][4]
        at = i * rows_h + 16 * place_of(i, slot) + 8 * kind
        value = stacked(part[at : at + 8, :])
        for e, copy in coming[i].get(node, []):
            copy.wait_recv()
            value = value + into[e].astype(F32)
        return value

    def scatter_send(i, e):
        at, out, into, rows = rings[i][1], rings[i][3], rings[i][4], rings[i][6]
        if e >= len(rows):
            return
        node, parent, cross, jump = rows[e]
        out[e] = summed(i, node).astype(BF16)
        copy = send(out.at[e], into.at[e], rs_s.at[i, e], rs_r.at[i, e], at(cross, -jump))
        coming[i].setdefault(parent, []).append((e, copy))
        sent.append(copy)

    def scatter_sends(start, stop):
        for e in range(start, stop):
            for i in (0, 1):
                scatter_send(i, e)

    leaves = LEAVES if nz == 8 or ny == 8 else 1
    scatter_sends(0, leaves)
    settled = len(sent)
    scatter_sends(leaves, max(leaves, 10))
    def in_bank_order(of_h, of_g):
        cut_h, cut_g = 16 * early[0], 16 * early[1]
        parts = [of_h[0:cut_h]] * (cut_h > 0) + [of_g[0:cut_g]] * (cut_g > 0)
        return jnp.transpose(jnp.concatenate(parts + [of_h[cut_h:], of_g[cut_g:]], axis=0))

    w_q = jnp.concatenate(
        [in_bank_order(w_own, w_g), in_bank_order(w_par, jnp.zeros((rows_g, rows_q), F32))], axis=0
    ).astype(BF16)
    for h in (0, 1):
        cols = slice(h * wh, (h + 1) * wh)
        both = jnp.dot(w_q, bank[:, cols], preferred_element_type=F32) * SCALE
        qf[:, cols] = both[0:rows_q]
        qs[:, cols] = both[rows_q:].astype(BF16)
    qg_send = send(qs, qr, core_s.at[3], core_r.at[3], other_core)
    for i in (0, 1):
        for copy in arrive[i].values():
            copy.wait_send()
    for copy in sent[:settled]:
        copy.wait_send()
    scatter_sends(max(leaves, 10), 13)
    qg_send.wait_recv()
    qg_ref[...] = qf[...] + qr[...].astype(F32)
    scatter_sends(13, 15)
    total = summed(0, (0, 0)) + summed(1, (0, 0))
    pg_ref[:, 0:wh] = total[0:8]
    pg_ref[:, wh:width] = total[8:16]
    for copy in sent[settled:] + [qg_send]:
        copy.wait_send()


def hand_over(qg_in, pg_in, loss_in, qg, pg, loss, sem):
    pairs = ((qg_in, qg), (pg_in, pg), (loss_in, loss))
    copies = [pltpu.make_async_copy(src, dst, sem.at[i]) for i, (src, dst) in enumerate(pairs)]
    for copy in copies:
        copy.start()
    for copy in copies:
        copy.wait()


def body(queries, passages, positive, neg_owner, neg_row):
    nblk, nshard = lax.axis_size("blk"), lax.axis_size("shard")
    ny, nz = nblk // 2, nshard // 4
    rows_q, width = queries.shape
    rows_p = passages.shape[0]
    negs = neg_owner.shape[1]
    wh = width // 2
    vmem = pl.BlockSpec(memory_space=pltpu.VMEM)
    anywhere = pl.BlockSpec(memory_space=pl.ANY)
    hbm = pl.BlockSpec(memory_space=pltpu.HBM)
    dma = pltpu.SemaphoreType.DMA
    top = max(ny, nz)
    scratch = [
        pltpu.VMEM((rows_q, width), F32),
        pltpu.VMEM((rows_p, width), F32),
        pltpu.VMEM((1, rows_q), I32),
        pltpu.VMEM((negs, rows_q), I32),
        pltpu.VMEM((negs, rows_q), I32),
        pltpu.VMEM((2 * rows_q, width), BF16),
        pltpu.VMEM((nz, 2, 16, wh), BF16),
        pltpu.VMEM((ny, 2, 16, wh), BF16),
        pltpu.VMEM((16 * (nz + ny), width), BF16),
        pltpu.VMEM((width, 2 * rows_q), BF16),
        pltpu.VMEM((16 * (nz + ny), 2 * rows_q), F32),
        pltpu.VMEM((16 * nz, 2 * rows_q), F32),
        pltpu.VMEM((2, 8, rows_q), I32),
        pltpu.VMEM((8, rows_q), I32),
        pltpu.VMEM((8, rows_q), F32),
        pltpu.VMEM((8, rows_q), F32),
        pltpu.VMEM((16 * (nz + ny), width), F32),
        pltpu.VMEM((2 * nz - 1, 16, wh), BF16),
        pltpu.VMEM((2 * nz - 1, 16, wh), BF16),
        pltpu.VMEM((2 * ny - 1, 16, wh), BF16),
        pltpu.VMEM((2 * ny - 1, 16, wh), BF16),
        pltpu.VMEM((rows_q, width), BF16),
        pltpu.VMEM((rows_q, width), BF16),
        dma((6,)),
        dma((2, 2 * top - 1)), dma((2, 2 * top - 1)),
        dma((4,)), dma((4,)),
        dma((2, 2 * top - 1)), dma((2, 2 * top - 1)),
    ]
    inputs = (queries, passages, positive.reshape(1, rows_q), neg_owner.T, neg_row.T)
    qg, pg, loss = pl.pallas_call(
        functools.partial(kernel, nblk, nshard),
        out_shape=(
            pltpu.VMEM((rows_q, width), F32),
            pltpu.VMEM((rows_p, width), F32),
            pltpu.VMEM((1, rows_q), F32),
        ),
        in_specs=[hbm] * 5,
        out_specs=(vmem,) * 3,
        scratch_shapes=scratch,
        compiler_params=pltpu.CompilerParams(
            collective_id=0, has_side_effects=True, vmem_limit_bytes=40 * 1024 * 1024
        ),
    )(*[pltpu.with_memory_space_constraint(a, pltpu.HBM) for a in inputs])
    qg, pg, loss = pl.pallas_call(
        hand_over,
        out_shape=tuple(jax.ShapeDtypeStruct(a.shape, a.dtype) for a in (qg, pg, loss)),
        in_specs=[anywhere] * 3,
        out_specs=(hbm,) * 3,
        scratch_shapes=[dma((3,))],
    )(*[pltpu.with_memory_space_constraint(a, pltpu.VMEM) for a in (qg, pg, loss)])
    return (qg, pg, loss.reshape(rows_q))


def solution(mesh):
    rows = P(("blk", "shard"), None)
    flat = P(("blk", "shard"))
    return jax.shard_map(
        body,
        mesh=mesh,
        in_specs=(rows, rows, flat, rows, rows),
        out_specs=(rows, rows, flat),
        check_vma=False,
    )
```
